32 devices in a mesh: rollout: 4 (over z), branch: 2 (over x), tensor: 4 (over y, core).
Axes of the slice: x: 2, y: 2, z: 4, core: 2. Of those that a mesh axis runs over, the one named last changes fastest.
Arguments:
- tokens: bfloat16 [8192, 2048], P(('rollout', 'branch')), parts along dimension 0, as said below
- parents: int32 [32], P('rollout'), parts along dimension 0, may hold values from 0 to 6, as said below
- lengths: int32 [32], P('rollout'), parts along dimension 0, may hold values from 128 to 256, as said below
- lin_qkv: bfloat16 [2048, 3, 1024], P(None, None, 'tensor'), may hold values from -0.125 to 0.125
- lin_gates: bfloat16 [2048, 2, 8], P(None, None, 'tensor'), as said below
- decay_rate: float32 [8], P('tensor'), as said below
- lin_out: bfloat16 [1024, 2048], P('tensor'), may hold values from -4 to 4
- norm_gain: float32 [2048], replicated, may hold values from 0.1 to 1.9
- att_q: bfloat16 [2048, 2048], P(None, 'tensor'), as said below
- att_kv: bfloat16 [2048, 2, 512], replicated, as said below
Outputs:
- lin_mixed: bfloat16 [8192, 2048], P(('rollout', 'branch', 'tensor')), parts along dimension 0
- att_out: bfloat16 [8192, 2048], P(('rollout', 'branch'), 'tensor'), parts along dimension 0
The draws below stay inside these ranges and needn't reach their ends.
There are 4 independent parts, one for each index of `rollout`. The reference program is written for one: setup_inputs(seed, part) draws one part's arguments, and reference() takes and returns one part's arrays. A program takes and returns all parts, laid end to end along the dimension named above; an argument that names none is the same for every part. Nothing has to cross between parts.
Inputs may be any that keep to these rules, and one draw needn't show every extreme that they name: parents[0] = 0 marks the root; every other branch's parent is an earlier branch; the last branch's parent is the branch just before it. `lengths`: a multiple of 128; some branch has 256 valid tokens and some has 128. `decay_rate`: positive. `tokens`: entries of order one. `lin_gates`: entries of order one over the square root of 2048. `att_q`: entries of order one over the square root of 2048. `att_kv`: entries of order one over the square root of 2048.
All inputs are finite; a program needn't handle non-finite values.
Results may differ from the reference program's by a relative error of at most 0.035.
Values may be sent and summed in bfloat16 or wider, within the bound.
A program may use at most 128 MiB of HBM per device.

```python
import math
import jax
import jax.numpy as jnp
from jax import lax

D = 2048
LIN_HEADS = 8
LIN_DIM = 128
Q_HEADS = 8
KV_HEADS = 2
ATT_DIM = 256
BLOCK = 64
TILE = 128
SEG = 256
SEGMENTS = 8
ROWS = 2048


token_shift = 0.5


write_bias = 2.2


def draw_parents(key, part):
    spine_key = jax.random.fold_in(key, 1)
    pick_key = jax.random.fold_in(key, 2)
    seg_ids = jnp.arange(SEGMENTS, dtype=jnp.int32)
    on_spine = (jax.random.randint(spine_key, (SEGMENTS,), 0, 4) < 3) | (seg_ids == 0) | (seg_ids >= SEGMENTS - 2)
    marks = jnp.where(on_spine, seg_ids, 0).astype(jnp.int32)
    latest = lax.cummax(marks, axis=0)
    previous = jnp.concatenate([jnp.zeros((1,), jnp.int32), latest[:-1].astype(jnp.int32)])
    upper = jnp.maximum(seg_ids, 1)
    chosen = jax.random.randint(pick_key, (SEGMENTS,), 0, upper).astype(jnp.int32)
    result = jnp.where(on_spine, previous, chosen)
    return jnp.where(seg_ids == 0, 0, result).astype(jnp.int32)


def draw_lengths(key, part):
    first_key = jax.random.fold_in(key, 11)
    second_key = jax.random.fold_in(key, 12)
    third_key = jax.random.fold_in(key, 13)
    seg_ids = jnp.arange(SEGMENTS)
    tiles = jax.random.randint(first_key, (SEGMENTS,), 1, SEG // TILE + 1) * TILE
    longest = jax.random.randint(second_key, (), 0, SEGMENTS)
    shortest = (longest + 1 + jax.random.randint(third_key, (), 0, SEGMENTS - 1)) % SEGMENTS
    chosen = jnp.where(seg_ids == longest, SEG, jnp.where(seg_ids == shortest, TILE, tiles))
    return chosen.astype(jnp.int32)


def draw_decay_rate(key, part):
    pick_key = jax.random.fold_in(key, 21)
    slow_key = jax.random.fold_in(key, 22)
    fast_key = jax.random.fold_in(key, 23)
    share = 0.5
    is_slow = jax.random.uniform(pick_key, (LIN_HEADS,), jnp.float32) < share
    slow_log = jax.random.uniform(slow_key, (LIN_HEADS,), jnp.float32, math.log(0.1), math.log(2.0))
    fast_log = jax.random.uniform(fast_key, (LIN_HEADS,), jnp.float32, math.log(0.02), math.log(0.06))
    slow_rate = jnp.exp(slow_log) / ROWS
    fast_rate = jnp.exp(fast_log)
    return jnp.where(is_slow, slow_rate, fast_rate).astype(jnp.float32)


def weight_noise(key, shape, fan_in):
    raw = jax.random.truncated_normal(key, -6.0, 6.0, shape, jnp.float32)
    return raw / math.sqrt(fan_in)


def draw_tokens(key, part):
    noise_key = jax.random.fold_in(key, 61)
    raw = jax.random.truncated_normal(noise_key, -6.0, 6.0, (ROWS, D), jnp.float32)
    return (raw + token_shift).astype(jnp.bfloat16)


def draw_lin_gates(key, part):
    noise = weight_noise(jax.random.fold_in(key, 51), (D, 2, LIN_HEADS), D)
    write_column = (jnp.arange(2) == 1).astype(jnp.float32)
    shift = write_bias / (token_shift * D)
    result = noise - shift * write_column[None, :, None]
    return result.astype(jnp.bfloat16)


def draw_att_q(key, part):
    result = weight_noise(jax.random.fold_in(key, 41), (D, Q_HEADS * ATT_DIM), D)
    return result.astype(jnp.bfloat16)


def draw_att_kv(key, part):
    result = weight_noise(jax.random.fold_in(key, 42), (D, 2, KV_HEADS * ATT_DIM), D)
    return result.astype(jnp.bfloat16)


def shard_levels(rng, extent, cuts, least, high):
    gain = 1.0
    for dim, parts in cuts:
        draws = jax.random.uniform(jax.random.fold_in(jax.random.fold_in(rng, 6), dim), (parts,), jnp.float32, least / len(cuts), high / len(cuts))
        gain = gain * jnp.repeat(jnp.exp(draws), extent[dim] // parts).reshape((-1,) + (1,) * (len(extent) - 1 - dim))
    return gain


def gaussian(rng, shape, scale, most, cuts=(), kind=jnp.bfloat16):
    loudness = shard_levels(rng, shape, cuts, -0.22, 0.18) if cuts else 1.0
    entries = jax.random.normal(rng, shape, jnp.float32) * scale * loudness
    return jnp.minimum(jnp.maximum(entries, -most), most).astype(kind)


def setup_inputs(seed: int = 0, part: int = 0) -> dict:
    key_of = jax.random.split(jax.random.key(seed), 11)
    part_keys = jax.random.split(jax.random.fold_in(key_of[10], part), 11)
    return {
        "tokens": draw_tokens(jax.random.fold_in(jax.random.fold_in(key_of[10], part), 71), part),
        "parents": draw_parents(jax.random.fold_in(jax.random.fold_in(key_of[10], part), 71), part),
        "lengths": draw_lengths(jax.random.fold_in(jax.random.fold_in(key_of[10], part), 71), part),
        "lin_qkv": gaussian(key_of[3], (D, 3, LIN_HEADS * LIN_DIM), D ** -0.5, 0.125, ((2, 4),)),
        "lin_gates": draw_lin_gates(jax.random.fold_in(key_of[10], 71), part),
        "decay_rate": draw_decay_rate(jax.random.fold_in(key_of[10], 71), part),
        "lin_out": gaussian(key_of[6], (LIN_HEADS * LIN_DIM, D), 2 ** -0.5, 4.0, ((0, 4),)),
        "norm_gain": jnp.clip(1.0 + 0.18 * jax.random.normal(key_of[7], (D,), jnp.float32), 0.1, 1.9),
        "att_q": draw_att_q(jax.random.fold_in(key_of[10], 71), part),
        "att_kv": draw_att_kv(jax.random.fold_in(key_of[10], 71), part),
    }


highest = lax.Precision.HIGHEST

def unit_rows(matrix):
    return matrix * lax.rsqrt(lax.optimization_barrier(jnp.sum(matrix * matrix, axis=-1, keepdims=True)) + 1e-06)

def ancestor_table(parent_map):
    count = parent_map.shape[0]

    def widen(counter, table):
        return parent_map + jnp.dot(parent_map, table, precision=highest)
    return lax.fori_loop(0, count - 1, widen, parent_map)

def block_terms(q_unit, k_unit, values, beta, log_decay):
    blocks = q_unit.shape[0] // BLOCK

    def split_block(array):
        shaped = array.reshape((blocks, BLOCK) + array.shape[1:])
        return jnp.swapaxes(shaped, 1, 2)
    queries = split_block(q_unit)
    keys_blk = split_block(k_unit)
    vals_blk = split_block(values)
    beta_blk = split_block(beta)
    decay_blk = jnp.cumsum(split_block(log_decay), axis=-1)
    final_decay = decay_blk[..., -1:]
    gap = decay_blk[..., :, None] - decay_blk[..., None, :]
    places = jnp.arange(BLOCK)
    strict = places[:, None] > places[None, :]
    inclusive = places[:, None] >= places[None, :]
    key_key = jnp.einsum('nhtd,nhsd->nhts', keys_blk, keys_blk, precision=highest)
    query_key = jnp.einsum('nhtd,nhsd->nhts', queries, keys_blk, precision=highest)
    lower_part = jnp.where(strict, beta_blk[..., :, None] * jnp.exp(jnp.where(strict, gap, 0.0)) * key_key, 0.0)
    system = lower_part + jnp.eye(BLOCK, dtype=lower_part.dtype)
    right_hand = jnp.concatenate([beta_blk[..., None] * vals_blk, (beta_blk * jnp.exp(decay_blk))[..., None] * keys_blk], axis=-1)
    solved = jax.scipy.linalg.solve_triangular(system, right_hand, lower=True, unit_diagonal=True)
    value_width = vals_blk.shape[-1]
    pseudo = solved[..., :value_width]
    weighted = solved[..., value_width:]
    carried_keys = jnp.exp(final_decay - decay_blk)[..., None] * keys_blk
    scaled_queries = jnp.exp(decay_blk)[..., None] * queries
    mixing = jnp.where(inclusive, jnp.exp(jnp.where(inclusive, gap, 0.0)) * query_key, 0.0)
    overall = jnp.exp(final_decay[..., 0])
    return (pseudo, weighted, carried_keys, scaled_queries, mixing, overall)

def run_outputs(initial, terms):

    def advance(current, block_part):
        pseudo, weighted, carried_keys, scaled_queries, mixing, overall = block_part
        update = pseudo - jnp.einsum('htk,hkm->htm', weighted, current, precision=highest)
        produced = jnp.einsum('htk,hkm->htm', scaled_queries, current, precision=highest)
        produced = produced + jnp.einsum('hts,hsm->htm', mixing, update, precision=highest)
        renewed = overall[:, None, None] * current + jnp.einsum('htk,htm->hkm', carried_keys, update, precision=highest)
        return (renewed, produced)
    final_state, produced = lax.scan(advance, initial, terms)
    blocks, head_count, block_len, value_width = produced.shape
    return (final_state, jnp.swapaxes(produced, 1, 2).reshape(blocks * block_len, head_count, value_width))

def reference(tokens, parents, lengths, lin_qkv, lin_gates, decay_rate, lin_out, norm_gain, att_q, att_kv):
    seg_ids = jnp.arange(SEGMENTS)
    parent_map = ((parents[:, None] == seg_ids[None, :]) & (seg_ids[:, None] > 0)).astype(jnp.float32)
    ancestors = (ancestor_table(parent_map) > 0.5).astype(jnp.int32)
    row_ids = jnp.arange(ROWS)
    row_seg = row_ids // SEG
    positions = row_ids % SEG
    row_limit = lax.optimization_barrier(jnp.sum(jnp.where(row_seg[:, None] == seg_ids[None, :], lengths[None, :], 0), axis=1))
    valid = positions < row_limit
    projected = jnp.dot(tokens.astype(jnp.float32), lin_qkv.reshape(D, -1).astype(jnp.float32), preferred_element_type=jnp.float32)
    projected = projected.reshape(ROWS, 3, LIN_HEADS, LIN_DIM)
    q_unit = unit_rows(projected[:, 0]) / math.sqrt(LIN_DIM)
    k_unit = unit_rows(projected[:, 1])
    values = projected[:, 2]
    gate_raw = jnp.dot(tokens.astype(jnp.float32), lin_gates.reshape(D, -1).astype(jnp.float32), preferred_element_type=jnp.float32).reshape(ROWS, 2, LIN_HEADS)
    beta = jnp.where(valid[:, None], jax.nn.sigmoid(gate_raw[:, 1]), 0.0)
    log_decay = jnp.where(valid[:, None], -decay_rate[None, :] * jax.nn.softplus(gate_raw[:, 0]), 0.0)
    ends = jnp.zeros((SEGMENTS, LIN_HEADS, LIN_DIM, LIN_DIM), jnp.float32)
    pieces = []
    for segment in range(SEGMENTS):
        lower_row = segment * SEG
        upper_row = lower_row + SEG
        terms = block_terms(q_unit[lower_row:upper_row], k_unit[lower_row:upper_row], values[lower_row:upper_row], beta[lower_row:upper_row], log_decay[lower_row:upper_row])
        if segment == 0:
            initial = jnp.zeros((LIN_HEADS, LIN_DIM, LIN_DIM), jnp.float32)
        else:
            initial = lax.dynamic_index_in_dim(ends, parents[segment], 0, keepdims=False)
        final_state, produced = run_outputs(initial, terms)
        ends = ends.at[segment].set(final_state)
        pieces.append(produced)
    lin_heads = jnp.concatenate(pieces, axis=0)
    lin_values = jnp.where(valid[:, None], lin_heads.reshape(ROWS, -1), 0.0).astype(jnp.bfloat16)
    mixed_sum = tokens.astype(jnp.float32) + jnp.dot(lin_values.astype(jnp.float32), lin_out.astype(jnp.float32), preferred_element_type=jnp.float32)
    lin_mixed = mixed_sum.astype(jnp.bfloat16)
    normed = (mixed_sum * lax.rsqrt(lax.optimization_barrier(jnp.mean(mixed_sum * mixed_sum, axis=-1, keepdims=True)) + 1e-06) * norm_gain).astype(jnp.bfloat16)
    att_queries = jnp.dot(normed.astype(jnp.float32), att_q.astype(jnp.float32), preferred_element_type=jnp.float32).astype(jnp.bfloat16)
    att_kvs = jnp.dot(normed.astype(jnp.float32), att_kv.reshape(D, -1).astype(jnp.float32), preferred_element_type=jnp.float32).astype(jnp.bfloat16)
    att_kvs = att_kvs.reshape(ROWS, 2, KV_HEADS, ATT_DIM)
    key_full = att_kvs[:, 0].astype(jnp.float32)
    value_full = att_kvs[:, 1].astype(jnp.float32)
    group = Q_HEADS // KV_HEADS
    key_valid = valid
    local_pos = jnp.arange(SEG)
    outputs = []
    for segment in range(SEGMENTS):
        lower_row = segment * SEG
        query_block = att_queries[lower_row:lower_row + SEG].astype(jnp.float32).reshape(SEG, KV_HEADS, group, ATT_DIM)
        scores = jnp.einsum('qcgd,kcd->cgqk', query_block, key_full, precision=highest) / math.sqrt(ATT_DIM)
        is_ancestor = ancestors[segment][row_seg] > 0
        own_branch = (row_seg == segment)[None, :] & (positions[None, :] <= local_pos[:, None])
        allowed = key_valid[None, :] & (is_ancestor[None, :] | own_branch)
        masked = jnp.where(allowed[None, None], scores, -1e+30)
        top = lax.optimization_barrier(jnp.max(masked, axis=-1, keepdims=True))
        numer = jnp.where(allowed[None, None], jnp.exp(scores - top), 0.0)
        denominators = lax.optimization_barrier(jnp.sum(numer, axis=-1))
        weights = numer.astype(jnp.bfloat16)
        weights = lax.optimization_barrier(weights).astype(jnp.float32)
        summed = jnp.einsum('cgqk,kcd->cgqd', weights, value_full, precision=highest)
        result = summed / denominators[..., None]
        result = jnp.transpose(result, (2, 0, 1, 3)).reshape(SEG, Q_HEADS * ATT_DIM)
        query_valid = valid[lower_row:lower_row + SEG]
        outputs.append(jnp.where(query_valid[:, None], result, 0.0).astype(jnp.bfloat16))
    att_out = jnp.concatenate(outputs, axis=0)
    return (lin_mixed, att_out)
```

```python
import functools
import math

import jax
import jax.numpy as jnp
from jax import lax
from jax.experimental import pallas as pl
from jax.experimental.pallas import tpu as pltpu
from jax.sharding import PartitionSpec as P

KV_HEADS = 2
ATT_DIM = 256
SEG = 256
MIB = 1024 * 1024

f32 = jnp.float32
bf16 = jnp.bfloat16
highest = lax.Precision.HIGHEST
MESH = pl.DeviceIdType.MESH

NN = (((1,), (0,)), ((), ()))
NT = (((1,), (1,)), ((), ()))
TN = (((0,), (0,)), ((), ()))


def dot1(a, b, dims=NN):
    return lax.dot_general(a, b, dims, preferred_element_type=f32)


def split(x):
    high = x.astype(bf16)
    return high, (x - high.astype(f32)).astype(bf16)


def dot3(a, b, dims=NN):
    (ah, al), (bh, bl) = a, b
    return dot1(ah, bh, dims) + (dot1(ah, bl, dims) + dot1(al, bh, dims))


def unit_rows(matrix):
    return matrix * lax.rsqrt(jnp.sum(matrix * matrix, axis=-1, keepdims=True) + 1e-06)


def ancestor_table(parent_map):
    count = parent_map.shape[0]

    def widen(counter, table):
        return parent_map + jnp.dot(parent_map, table, precision=highest)

    return lax.fori_loop(0, count - 1, widen, parent_map)


def delta_kernel(heads, dim, lens_ref, rate_ref, tok_ref, w_ref, o1_ref, q2_ref, a_ref, b_ref):
    limit = lens_ref[pl.program_id(0)]
    proj = dot1(tok_ref[...], w_ref[...])
    rows = lax.broadcasted_iota(jnp.int32, (SEG, SEG), 0)
    cols = lax.broadcasted_iota(jnp.int32, (SEG, SEG), 1)
    strict = rows > cols
    inclusive = rows >= cols
    tril = inclusive.astype(f32)
    valid = lax.broadcasted_iota(jnp.int32, (SEG, 1), 0) < limit
    width = heads * dim
    eye = (rows == cols).astype(f32)
    parts = []
    for h in range(heads):
        q = unit_rows(proj[:, h * dim : (h + 1) * dim]) / math.sqrt(dim)
        k = unit_rows(proj[:, width + h * dim : width + (h + 1) * dim])
        v = proj[:, 2 * width + h * dim : 2 * width + (h + 1) * dim]
        g0 = proj[:, 3 * width + h : 3 * width + h + 1]
        g1 = proj[:, 3 * width + heads + h : 3 * width + heads + h + 1]
        beta = jnp.where(valid, 1.0 / (1.0 + jnp.exp(-g1)), 0.0)
        soft = jnp.maximum(g0, 0.0) + jnp.log1p(jnp.exp(-jnp.abs(g0)))
        step = jnp.where(valid, -rate_ref[h] * soft, 0.0)
        total = lax.dot_general(
            tril, jnp.broadcast_to(step, (SEG, dim)), NN, precision=highest,
            preferred_element_type=f32,
        )
        col = total[:, :1]
        row = total.T[:1, :]
        decay = jnp.exp(jnp.where(inclusive, col - row, 0.0))
        ks = split(k)
        key_key = dot3(ks, ks, NT)
        query_key = dot3(split(q), ks, NT)
        lower = jnp.where(strict, beta * decay * key_key, 0.0)
        mixing = jnp.where(inclusive, decay * query_key, 0.0)
        grown = jnp.exp(col)
        right = jnp.concatenate([beta * v, (beta * grown) * k], axis=1)
        last = total[SEG - 1 :, :]
        carried = jnp.exp(last - total) * k
        parts.append([lower, mixing, right, carried, grown * q, jnp.exp(last)])
    inverses = [eye - jnp.where(rows // 2 == cols // 2, p[0], 0.0) for p in parts]
    size = 2
    while size < SEG:
        pair = (rows // (2 * size) == cols // (2 * size)) & (rows // size != cols // size)
        halves = [split(x) for x in inverses]
        inner = [
            split(dot3(split(jnp.where(pair, p[0], 0.0)), x)) for p, x in zip(parts, halves)
        ]
        inverses = [x - dot3(xs, y) for x, xs, y in zip(inverses, halves, inner)]
        size *= 2
    small_eye = eye[:dim, :dim]
    for h in range(heads):
        lower, mixing, right, carried, queries, overall = parts[h]
        solved = split(dot3(split(inverses[h]), split(right)))
        out = dot3(split(mixing), solved)
        ends = dot3(split(carried), solved, TN)
        o1_ref[:, h * dim : (h + 1) * dim] = jnp.where(valid, out[:, :dim], 0.0)
        q2_ref[:, h * dim : (h + 1) * dim] = jnp.where(valid, queries - out[:, dim:], 0.0)
        b_ref[0, h] = ends[:, :dim]
        a_ref[0, h] = overall * small_eye - ends[:, dim:]


def delta_terms(tokens, weights, own_lengths, decay_rate, dim):
    heads = decay_rate.shape[0]
    rows, model = tokens.shape
    count = rows // SEG
    maps = jax.ShapeDtypeStruct((count, heads, dim, dim), f32)
    flat = jax.ShapeDtypeStruct((rows, heads * dim), f32)
    smem = pl.BlockSpec(memory_space=pltpu.SMEM)
    return pl.pallas_call(
        functools.partial(delta_kernel, heads, dim),
        grid=(count,),
        in_specs=[
            smem,
            smem,
            pl.BlockSpec((SEG, model), lambda s: (s, 0)),
            pl.BlockSpec(weights.shape, lambda s: (0, 0)),
        ],
        out_specs=[
            pl.BlockSpec((SEG, heads * dim), lambda s: (s, 0)),
            pl.BlockSpec((SEG, heads * dim), lambda s: (s, 0)),
            pl.BlockSpec((1, heads, dim, dim), lambda s: (s, 0, 0, 0)),
            pl.BlockSpec((1, heads, dim, dim), lambda s: (s, 0, 0, 0)),
        ],
        out_shape=[flat, flat, maps, maps],
        compiler_params=pltpu.CompilerParams(vmem_limit_bytes=40 * MIB),
    )(own_lengths, decay_rate, tokens, weights)


def mix_kernel(
    branches, tensors, parents_ref, a_ref, b_ref, o1_ref, q2_ref, lin_out_ref, tok_ref, gain_ref,
    mixed_ref, normed_ref,
    ends, ends16, starts, lin, total, end_send, end_recv, near_send, near_recv, far_send, far_recv,
    pass_send, pass_recv,
):
    me_b = lax.axis_index("branch")
    me_t = lax.axis_index("tensor")
    count, heads, dim, _ = a_ref.shape
    model = tok_ref.shape[1]
    chunk = mixed_ref.shape[0]
    chunks = lin.shape[1] // chunk
    width = heads * dim
    chips = tensors // 2
    chip, core = me_t // 2, me_t % 2
    partner = chip * 2 + (1 - core)
    ends[...] = jnp.zeros_like(ends)

    def far_of(f):
        return lax.rem(chip + 1 + f, chips)

    barrier = pltpu.get_barrier_semaphore()
    for d in range(1, branches):
        pl.semaphore_signal(
            barrier, inc=1, device_id={"branch": lax.rem(me_b + d, branches)}, device_id_type=MESH
        )
    pl.semaphore_signal(barrier, inc=1, device_id={"tensor": partner}, device_id_type=MESH)
    for f in range(chips - 1):
        pl.semaphore_signal(
            barrier, inc=1, device_id={"tensor": far_of(f) * 2 + core}, device_id_type=MESH
        )
    pl.semaphore_wait(barrier, branches - 1 + chips)

    first = me_b * count

    def end_copy(j, peer):
        return pltpu.make_async_remote_copy(
            src_ref=ends16.at[first + j], dst_ref=ends16.at[first + j],
            send_sem=end_send.at[j, peer], recv_sem=end_recv.at[first + j],
            device_id={"branch": peer}, device_id_type=MESH,
        )

    def take_end(s, carry):
        pltpu.make_async_remote_copy(
            src_ref=ends16.at[s], dst_ref=ends16.at[s],
            send_sem=end_send.at[0, 0], recv_sem=end_recv.at[s],
            device_id={"branch": lax.rem(me_b + 1, branches)}, device_id_type=MESH,
        ).wait_recv()
        ends[s] = ends16[s].astype(f32)
        return carry

    lax.fori_loop(0, first, take_end, 0)

    def advance(j, carry):
        s = first + j
        start = ends[parents_ref[s]]
        start = jnp.where(s > 0, start, jnp.zeros_like(start))
        starts[j] = start
        for h in range(heads):
            done = dot3(split(a_ref[j, h]), split(start[h])) + b_ref[j, h]
            ends[s, h] = done
            ends16[s, h] = done.astype(bf16)
        for peer in range(1, branches):
            @pl.when(me_b < peer)
            def _():
                end_copy(j, peer).start()
        return carry

    lax.fori_loop(0, count, advance, 0)

    def rows_of(i):
        return pl.ds(pl.multiple_of(i * chunk, chunk), chunk)

    def near_copy(i):
        return pltpu.make_async_remote_copy(
            src_ref=lin.at[me_t, rows_of(i)], dst_ref=lin.at[me_t, rows_of(i)],
            send_sem=near_send.at[i], recv_sem=near_recv.at[i],
            device_id={"tensor": partner}, device_id_type=MESH,
        )

    def far_copy(i, f):
        return pltpu.make_async_remote_copy(
            src_ref=lin.at[me_t, rows_of(i)], dst_ref=lin.at[me_t, rows_of(i)],
            send_sem=far_send.at[i, f], recv_sem=far_recv.at[i, f],
            device_id={"tensor": far_of(f) * 2 + core}, device_id_type=MESH,
        )

    def pass_copy(i, f):
        source = lax.rem(chip + chips - 1 - f, chips) * 2 + core
        return pltpu.make_async_remote_copy(
            src_ref=lin.at[source, rows_of(i)], dst_ref=lin.at[source, rows_of(i)],
            send_sem=pass_send.at[i, f], recv_sem=pass_recv.at[i, f],
            device_id={"tensor": partner}, device_id_type=MESH,
        )

    def produce(i, carry):
        j = (i * chunk) // SEG
        for h in range(heads):
            cols = slice(h * dim, (h + 1) * dim)
            out = o1_ref[rows_of(i), cols] + dot3(
                split(q2_ref[rows_of(i), cols]), split(starts[j, h])
            )
            lin[me_t, rows_of(i), cols] = out.astype(bf16)
        for f in range(chips - 1):
            far_copy(i, f).start()
        near_copy(i).start()
        return carry

    lax.fori_loop(0, chunks, produce, 0)

    def forward(i, carry):
        for f in range(chips - 1):
            far_copy(i, f).wait_recv()
            pass_copy(i, f).start()
        return carry

    tile = 512

    def mix(i, carry):
        forward(i, 0)
        near_copy(i).wait_recv()
        for f in range(chips - 1):
            pass_copy(i, f).wait_recv()

        def column(n, squares):
            cols = pl.ds(pl.multiple_of(n * tile, tile), tile)
            part = tok_ref[rows_of(i), cols].astype(f32)
            for t in range(tensors):
                part = part + dot1(
                    lin[t, rows_of(i), :], lin_out_ref[t * width : (t + 1) * width, cols]
                )
            total[:, cols] = part
            return squares + jnp.sum(part * part, axis=1, keepdims=True)

        squares = lax.fori_loop(0, model // tile, column, jnp.zeros((chunk, 1), f32))
        scale = lax.rsqrt(squares / model + 1e-06)
        normed_ref[rows_of(i), :] = (total[...] * scale * gain_ref[...]).astype(bf16)

        @pl.when(i == me_t)
        def _():
            mixed_ref[...] = total[...].astype(bf16)

        return carry

    lax.fori_loop(0, chunks, mix, 0)

    def finish(i, carry):
        near_copy(i).wait_send()
        for f in range(chips - 1):
            far_copy(i, f).wait_send()
            pass_copy(i, f).wait_send()
        return carry

    lax.fori_loop(0, chunks, finish, 0)

    def finish_ends(j, carry):
        for peer in range(1, branches):
            @pl.when(me_b < peer)
            def _():
                end_copy(j, peer).wait_send()
        return carry

    lax.fori_loop(0, count, finish_ends, 0)


def mix_rows(parents, amap, bmap, o1, q2, lin_out, tokens, gain):
    branches, tensors = lax.axis_size("branch"), lax.axis_size("tensor")
    count, heads, dim, _ = amap.shape
    rows, model = tokens.shape
    chunk = rows // tensors
    chunks = tensors
    segments = branches * count
    fars = max(tensors // 2 - 1, 1)
    vmem = pl.BlockSpec(memory_space=pltpu.VMEM)
    dma = pltpu.SemaphoreType.DMA
    return pl.pallas_call(
        functools.partial(mix_kernel, branches, tensors),
        in_specs=[pl.BlockSpec(memory_space=pltpu.SMEM)] + [vmem] * 7,
        out_specs=[vmem, vmem],
        out_shape=[
            jax.ShapeDtypeStruct((chunk, model), bf16),
            jax.ShapeDtypeStruct((rows, model), bf16),
        ],
        scratch_shapes=[
            pltpu.VMEM((segments, heads, dim, dim), f32),
            pltpu.VMEM((segments, heads, dim, dim), bf16),
            pltpu.VMEM((count, heads, dim, dim), f32),
            pltpu.VMEM((tensors, rows, heads * dim), bf16),
            pltpu.VMEM((chunk, model), f32),
            dma((count, branches)),
            dma((segments,)),
            dma((chunks,)),
            dma((chunks,)),
            dma((chunks, fars)),
            dma((chunks, fars)),
            dma((chunks, fars)),
            dma((chunks, fars)),
        ],
        compiler_params=pltpu.CompilerParams(
            collective_id=0, has_side_effects=True, vmem_limit_bytes=56 * MIB
        ),
    )(parents, amap, bmap, o1, q2, lin_out, tokens, gain)


def on_device(
    tokens, parents, lengths, lin_qkv, lin_gates, decay_rate, lin_out, norm_gain, att_q, att_kv
):
    branch_idx = lax.axis_index("branch")
    tensor_count = lax.axis_size("tensor")
    tensor_idx = lax.axis_index("tensor")
    local_rows, model_width = tokens.shape
    local_count = local_rows // SEG
    segment_count = lax.axis_size("branch") * local_count
    local_heads = decay_rate.shape[0]
    head_dim = lin_qkv.shape[2] // local_heads
    att_dim = ATT_DIM
    first_seg = branch_idx * local_count
    full_out = lax.all_gather(lin_out, "tensor", axis=0, tiled=True)
    own_lengths = lax.dynamic_slice_in_dim(lengths, first_seg, local_count, 0)
    weights = jnp.concatenate(
        [
            lin_qkv.reshape(model_width, -1),
            lin_gates.reshape(model_width, -1),
            jnp.zeros((model_width, 128 - 2 * local_heads), bf16),
        ],
        axis=1,
    )
    o1, q2, amap, bmap = delta_terms(tokens, weights, own_lengths, decay_rate, head_dim)
    lin_mixed, normed = mix_rows(
        parents, amap, bmap, o1, q2, full_out, tokens, norm_gain[None, :]
    )
    return attend(lin_mixed, normed, parents, lengths, att_q, att_kv)


def attend(lin_mixed, normed, parents, lengths, att_q, att_kv):
    branch_idx = lax.axis_index("branch")
    tensor_count = lax.axis_size("tensor")
    tensor_idx = lax.axis_index("tensor")
    local_rows, model_width = normed.shape
    local_count = local_rows // SEG
    segment_count = lax.axis_size("branch") * local_count
    first_seg = branch_idx * local_count
    att_dim = ATT_DIM
    seg_ids = jnp.arange(segment_count)
    local_flag = seg_ids[None, :] == (first_seg + jnp.arange(local_count))[:, None]
    own_lengths = jnp.sum(jnp.where(local_flag, lengths[None, :], 0), axis=1)
    valid = (jnp.arange(SEG)[None, :] < own_lengths[:, None]).reshape(local_rows)
    row_local = jnp.arange(local_rows)
    query_seg = first_seg + row_local // SEG
    query_pos = row_local % SEG
    parent_map = ((parents[:, None] == seg_ids[None, :]) & (seg_ids[:, None] > 0)).astype(f32)
    ancestry = ancestor_table(parent_map)
    local_anc = (jnp.dot(local_flag.astype(f32), ancestry, precision=highest) > 0.5).astype(f32)
    query_anc = jnp.repeat(local_anc, SEG, axis=0)
    local_q = att_q.shape[1] // att_dim
    kv_head = tensor_idx // (tensor_count // KV_HEADS)
    scale_factor = 1.0 / math.sqrt(att_dim)
    own_kv = lax.dynamic_slice_in_dim(att_kv, kv_head * att_dim, att_dim, 2)
    kv = jnp.dot(normed, own_kv.reshape(model_width, -1), preferred_element_type=f32).astype(bf16)
    full_kv = lax.all_gather(kv, "branch", axis=0, tiled=True)
    key_part, value_part = full_kv[:, :att_dim], full_kv[:, att_dim:]
    queries = jnp.dot(normed, att_q, preferred_element_type=f32).astype(bf16)
    queries = queries.reshape(local_rows, local_q, att_dim)
    global_rows = jnp.arange(key_part.shape[0])
    key_seg = global_rows // SEG
    key_pos = global_rows % SEG
    match = key_seg[:, None] == seg_ids[None, :]
    key_limit = jnp.sum(jnp.where(match, lengths[None, :], 0), axis=1)
    key_ancestor = jnp.dot(query_anc, match.astype(f32).T, precision=highest) > 0.5
    own_branch = (key_seg[None, :] == query_seg[:, None]) & (key_pos[None, :] <= query_pos[:, None])
    allowed = (key_pos < key_limit)[None, :] & (key_ancestor | own_branch)
    scores = (
        jnp.einsum("qhd,kd->hqk", queries, key_part, preferred_element_type=f32) * scale_factor
    )
    top = jnp.max(jnp.where(allowed[None], scores, -1e30), axis=-1)
    numer = jnp.where(allowed[None], jnp.exp(scores - top[..., None]), 0.0)
    sums = jnp.sum(numer, axis=-1)
    accum = jnp.einsum("hqk,kd->hqd", numer.astype(bf16), value_part, preferred_element_type=f32)
    result = accum / sums[..., None]
    result = jnp.swapaxes(result, 0, 1).reshape(local_rows, local_q * att_dim)
    att_out = jnp.where(valid[:, None], result, 0.0).astype(bf16)
    return (lin_mixed, att_out)


def solution(mesh):
    placed = (
        P(("rollout", "branch"), None),
        P("rollout"),
        P("rollout"),
        P(None, None, "tensor"),
        P(None, None, "tensor"),
        P("tensor"),
        P("tensor", None),
        P(),
        P(None, "tensor"),
        P(),
    )
    return jax.shard_map(
        on_device,
        mesh=mesh,
        in_specs=placed,
        out_specs=(P(("rollout", "branch", "tensor"), None), P(("rollout", "branch"), "tensor")),
        check_vma=False,
    )
```

```python
import functools
import math

import jax
import jax.numpy as jnp
from jax import lax
from jax.experimental import pallas as pl
from jax.experimental.pallas import tpu as pltpu
from jax.sharding import PartitionSpec as P

KV_HEADS = 2
ATT_DIM = 256
SEG = 256
MIB = 1024 * 1024

f32 = jnp.float32
bf16 = jnp.bfloat16
highest = lax.Precision.HIGHEST
MESH = pl.DeviceIdType.MESH

NN = (((1,), (0,)), ((), ()))
NT = (((1,), (1,)), ((), ()))
TN = (((0,), (0,)), ((), ()))


def dot1(a, b, dims=NN):
    return lax.dot_general(a, b, dims, preferred_element_type=f32)


def split(x):
    high = x.astype(bf16)
    return high, (x - high.astype(f32)).astype(bf16)


def dot3(a, b, dims=NN):
    (ah, al), (bh, bl) = a, b
    ax, bx = dims[0][0][0], dims[0][1][0]
    left = jnp.concatenate([ah, ah, al], axis=ax)
    right = jnp.concatenate([bh, bl, bh], axis=bx)
    return dot1(left, right, dims)


def unit_rows(matrix):
    return matrix * lax.rsqrt(jnp.sum(matrix * matrix, axis=-1, keepdims=True) + 1e-06)


def ancestor_table(parent_map):
    count = parent_map.shape[0]

    def widen(counter, table):
        return parent_map + jnp.dot(parent_map, table, precision=highest)

    return lax.fori_loop(0, count - 1, widen, parent_map)


def delta_kernel(
    heads, dim, per, lens_ref, rate_ref, tok_ref, w_ref, o1_ref, q2_ref, a_ref, b_ref
):
    proj_all = dot1(tok_ref[...], w_ref[...])
    half = SEG // 2
    rows = lax.broadcasted_iota(jnp.int32, (SEG, SEG), 0)
    cols = lax.broadcasted_iota(jnp.int32, (SEG, SEG), 1)
    strict = rows > cols
    inclusive = rows >= cols
    tril = inclusive.astype(f32)
    hrows = lax.broadcasted_iota(jnp.int32, (half, half), 0)
    hcols = lax.broadcasted_iota(jnp.int32, (half, half), 1)
    places = lax.broadcasted_iota(jnp.int32, (SEG, 1), 0)
    width = heads * dim
    eye = (hrows == hcols).astype(f32)
    parts = []
    for g in range(per):
        valid = places < lens_ref[pl.program_id(0) * per + g]
        proj = proj_all[g * SEG : (g + 1) * SEG]
        for h in range(heads):
            q = unit_rows(proj[:, h * dim : (h + 1) * dim]) / math.sqrt(dim)
            k = unit_rows(proj[:, width + h * dim : width + (h + 1) * dim])
            v = proj[:, 2 * width + h * dim : 2 * width + (h + 1) * dim]
            g0 = proj[:, 3 * width + h : 3 * width + h + 1]
            g1 = proj[:, 3 * width + heads + h : 3 * width + heads + h + 1]
            beta = jnp.where(valid, 1.0 / (1.0 + jnp.exp(-g1)), 0.0)
            soft = jnp.maximum(g0, 0.0) + jnp.log1p(jnp.exp(-jnp.abs(g0)))
            step = jnp.where(valid, -rate_ref[h] * soft, 0.0)
            total = lax.dot_general(
                tril, jnp.broadcast_to(step, (SEG, dim)), NN, precision=highest,
                preferred_element_type=f32,
            )
            col = total[:, :1]
            row = total.T[:1, :]
            decay = jnp.exp(jnp.where(inclusive, col - row, 0.0))
            ks = split(k)
            key_key = dot3(ks, ks, NT)
            query_key = dot3(split(q), ks, NT)
            lower = jnp.where(strict, beta * decay * key_key, 0.0)
            mixing = jnp.where(inclusive, decay * query_key, 0.0)
            grown = jnp.exp(col)
            right = jnp.concatenate([beta * v, (beta * grown) * k], axis=1)
            last = total[SEG - 1 :, :]
            carried = jnp.exp(last - total) * k
            parts.append([lower, mixing, right, carried, grown * q, jnp.exp(last), valid])
    lowers = [
        p[0][c * half : (c + 1) * half, c * half : (c + 1) * half] for p in parts for c in range(2)
    ]
    inverses = [eye - jnp.where(hrows // 2 == hcols // 2, x, 0.0) for x in lowers]
    size = 2
    while size < half:
        pair = (hrows // (2 * size) == hcols // (2 * size)) & (hrows // size != hcols // size)
        halves = [split(x) for x in inverses]
        inner = [
            split(dot3(split(jnp.where(pair, x, 0.0)), y)) for x, y in zip(lowers, halves)
        ]
        inverses = [x - dot3(xs, y) for x, xs, y in zip(inverses, halves, inner)]
        size *= 2
    inverses = [split(x) for x in inverses]
    for g in range(per):
        for h in range(heads):
            n = g * heads + h
            lower, mixing, right, carried, queries, overall, valid = parts[n]
            upper = dot3(inverses[2 * n], split(right[:half]))
            rest = right[half:] - dot3(split(lower[half:, :half]), split(upper))
            bottom = dot3(inverses[2 * n + 1], split(rest))
            solved = split(jnp.concatenate([upper, bottom], axis=0))
            out = dot3(split(mixing), solved)
            ends = dot3(split(carried), solved, TN)
            at = slice(g * SEG, (g + 1) * SEG)
            o1_ref[at, h * dim : (h + 1) * dim] = jnp.where(valid, out[:, :dim], 0.0)
            q2_ref[at, h * dim : (h + 1) * dim] = jnp.where(valid, queries - out[:, dim:], 0.0)
            b_ref[g, h] = ends[:, :dim]
            a_ref[g, h] = overall * eye - ends[:, dim:]


def delta_terms(tokens, weights, own_lengths, decay_rate, dim):
    heads = decay_rate.shape[0]
    rows, model = tokens.shape
    count = rows // SEG
    per = 2 - count % 2
    maps = jax.ShapeDtypeStruct((count, heads, dim, dim), f32)
    flat = jax.ShapeDtypeStruct((rows, heads * dim), f32)
    smem = pl.BlockSpec(memory_space=pltpu.SMEM)
    return pl.pallas_call(
        functools.partial(delta_kernel, heads, dim, per),
        grid=(count // per,),
        in_specs=[
            smem,
            smem,
            pl.BlockSpec((per * SEG, model), lambda s: (s, 0)),
            pl.BlockSpec(weights.shape, lambda s: (0, 0)),
        ],
        out_specs=[
            pl.BlockSpec((per * SEG, heads * dim), lambda s: (s, 0)),
            pl.BlockSpec((per * SEG, heads * dim), lambda s: (s, 0)),
            pl.BlockSpec((per, heads, dim, dim), lambda s: (s, 0, 0, 0)),
            pl.BlockSpec((per, heads, dim, dim), lambda s: (s, 0, 0, 0)),
        ],
        out_shape=[flat, flat, maps, maps],
        compiler_params=pltpu.CompilerParams(vmem_limit_bytes=48 * MIB),
    )(own_lengths, decay_rate, tokens, weights)


def mix_kernel(
    branches, tensors, parents_ref, a_ref, b_ref, o1_ref, q2_ref, lin_out_ref, tok_ref, gain_ref,
    mixed_ref, normed_ref,
    ends, ends16, starts, lin, total, end_send, end_recv, near_send, near_recv, far_send, far_recv,
    pass_send, pass_recv,
):
    me_b = lax.axis_index("branch")
    me_t = lax.axis_index("tensor")
    count, heads, dim, _ = a_ref.shape
    model = tok_ref.shape[1]
    chunk = mixed_ref.shape[0]
    chunks = lin.shape[1] // chunk
    width = heads * dim
    chips = tensors // 2
    chip, core = me_t // 2, me_t % 2
    partner = chip * 2 + (1 - core)
    ends[...] = jnp.zeros_like(ends)

    def far_of(f):
        return lax.rem(chip + 1 + f, chips)

    barrier = pltpu.get_barrier_semaphore()
    for d in range(1, branches):
        pl.semaphore_signal(
            barrier, inc=1, device_id={"branch": lax.rem(me_b + d, branches)}, device_id_type=MESH
        )
    pl.semaphore_signal(barrier, inc=1, device_id={"tensor": partner}, device_id_type=MESH)
    for f in range(chips - 1):
        pl.semaphore_signal(
            barrier, inc=1, device_id={"tensor": far_of(f) * 2 + core}, device_id_type=MESH
        )
    pl.semaphore_wait(barrier, branches - 1 + chips)

    first = me_b * count

    def end_copy(j, peer):
        return pltpu.make_async_remote_copy(
            src_ref=ends16.at[first + j], dst_ref=ends16.at[first + j],
            send_sem=end_send.at[j, peer], recv_sem=end_recv.at[first + j],
            device_id={"branch": peer}, device_id_type=MESH,
        )

    def take_end(s, carry):
        pltpu.make_async_remote_copy(
            src_ref=ends16.at[s], dst_ref=ends16.at[s],
            send_sem=end_send.at[0, 0], recv_sem=end_recv.at[s],
            device_id={"branch": lax.rem(me_b + 1, branches)}, device_id_type=MESH,
        ).wait_recv()
        ends[s] = ends16[s].astype(f32)
        return carry

    lax.fori_loop(0, first, take_end, 0)

    def advance(j, carry):
        s = first + j
        start = ends[parents_ref[s]]
        start = jnp.where(s > 0, start, jnp.zeros_like(start))
        starts[j] = start
        for h in range(heads):
            done = dot3(split(a_ref[j, h]), split(start[h])) + b_ref[j, h]
            ends[s, h] = done
            ends16[s, h] = done.astype(bf16)
        for peer in range(1, branches):
            @pl.when(me_b < peer)
            def _():
                end_copy(j, peer).start()
        return carry

    lax.fori_loop(0, count, advance, 0)

    def rows_of(i):
        return pl.ds(pl.multiple_of(i * chunk, chunk), chunk)

    def near_copy(i):
        return pltpu.make_async_remote_copy(
            src_ref=lin.at[me_t, rows_of(i)], dst_ref=lin.at[me_t, rows_of(i)],
            send_sem=near_send.at[i], recv_sem=near_recv.at[i],
            device_id={"tensor": partner}, device_id_type=MESH,
        )

    def far_copy(i, f):
        return pltpu.make_async_remote_copy(
            src_ref=lin.at[me_t, rows_of(i)], dst_ref=lin.at[me_t, rows_of(i)],
            send_sem=far_send.at[i, f], recv_sem=far_recv.at[i, f],
            device_id={"tensor": far_of(f) * 2 + core}, device_id_type=MESH,
        )

    def pass_copy(i, f):
        source = lax.rem(chip + chips - 1 - f, chips) * 2 + core
        return pltpu.make_async_remote_copy(
            src_ref=lin.at[source, rows_of(i)], dst_ref=lin.at[source, rows_of(i)],
            send_sem=pass_send.at[i, f], recv_sem=pass_recv.at[i, f],
            device_id={"tensor": partner}, device_id_type=MESH,
        )

    def produce(i, carry):
        j = (i * chunk) // SEG
        for h in range(heads):
            cols = slice(h * dim, (h + 1) * dim)
            out = o1_ref[rows_of(i), cols] + dot3(
                split(q2_ref[rows_of(i), cols]), split(starts[j, h])
            )
            lin[me_t, rows_of(i), cols] = out.astype(bf16)
        for f in range(chips - 1):
            far_copy(i, f).start()
        near_copy(i).start()
        return carry

    lax.fori_loop(0, chunks, produce, 0)

    def forward(i, carry):
        for f in range(chips - 1):
            far_copy(i, f).wait_recv()
            pass_copy(i, f).start()
        return carry

    tile = 512

    def mix(i, carry):
        forward(i, 0)
        near_copy(i).wait_recv()
        for f in range(chips - 1):
            pass_copy(i, f).wait_recv()

        def column(n, squares):
            cols = pl.ds(pl.multiple_of(n * tile, tile), tile)
            part = tok_ref[rows_of(i), cols].astype(f32)
            for t in range(tensors):
                part = part + dot1(
                    lin[t, rows_of(i), :], lin_out_ref[t * width : (t + 1) * width, cols]
                )
            total[:, cols] = part
            return squares + jnp.sum(part * part, axis=1, keepdims=True)

        squares = lax.fori_loop(0, model // tile, column, jnp.zeros((chunk, 1), f32))
        scale = lax.rsqrt(squares / model + 1e-06)
        normed_ref[rows_of(i), :] = (total[...] * scale * gain_ref[...]).astype(bf16)

        @pl.when(i == me_t)
        def _():
            mixed_ref[...] = total[...].astype(bf16)

        return carry

    lax.fori_loop(0, chunks, mix, 0)

    def finish(i, carry):
        near_copy(i).wait_send()
        for f in range(chips - 1):
            far_copy(i, f).wait_send()
            pass_copy(i, f).wait_send()
        return carry

    lax.fori_loop(0, chunks, finish, 0)

    def finish_ends(j, carry):
        for peer in range(1, branches):
            @pl.when(me_b < peer)
            def _():
                end_copy(j, peer).wait_send()
        return carry

    lax.fori_loop(0, count, finish_ends, 0)


def mix_rows(parents, amap, bmap, o1, q2, lin_out, tokens, gain):
    branches, tensors = lax.axis_size("branch"), lax.axis_size("tensor")
    count, heads, dim, _ = amap.shape
    rows, model = tokens.shape
    chunk = rows // tensors
    chunks = tensors
    segments = branches * count
    fars = max(tensors // 2 - 1, 1)
    vmem = pl.BlockSpec(memory_space=pltpu.VMEM)
    dma = pltpu.SemaphoreType.DMA
    return pl.pallas_call(
        functools.partial(mix_kernel, branches, tensors),
        in_specs=[pl.BlockSpec(memory_space=pltpu.SMEM)] + [vmem] * 7,
        out_specs=[vmem, vmem],
        out_shape=[
            jax.ShapeDtypeStruct((chunk, model), bf16),
            jax.ShapeDtypeStruct((rows, model), bf16),
        ],
        scratch_shapes=[
            pltpu.VMEM((segments, heads, dim, dim), f32),
            pltpu.VMEM((segments, heads, dim, dim), bf16),
            pltpu.VMEM((count, heads, dim, dim), f32),
            pltpu.VMEM((tensors, rows, heads * dim), bf16),
            pltpu.VMEM((chunk, model), f32),
            dma((count, branches)),
            dma((segments,)),
            dma((chunks,)),
            dma((chunks,)),
            dma((chunks, fars)),
            dma((chunks, fars)),
            dma((chunks, fars)),
            dma((chunks, fars)),
        ],
        compiler_params=pltpu.CompilerParams(
            collective_id=0, has_side_effects=True, vmem_limit_bytes=56 * MIB
        ),
    )(parents, amap, bmap, o1, q2, lin_out, tokens, gain)


def on_device(
    tokens, parents, lengths, lin_qkv, lin_gates, decay_rate, lin_out, norm_gain, att_q, att_kv
):
    branch_idx = lax.axis_index("branch")
    tensor_count = lax.axis_size("tensor")
    tensor_idx = lax.axis_index("tensor")
    local_rows, model_width = tokens.shape
    local_count = local_rows // SEG
    segment_count = lax.axis_size("branch") * local_count
    local_heads = decay_rate.shape[0]
    head_dim = lin_qkv.shape[2] // local_heads
    att_dim = ATT_DIM
    first_seg = branch_idx * local_count
    full_out = lax.all_gather(lin_out, "tensor", axis=0, tiled=True)
    own_lengths = lax.dynamic_slice_in_dim(lengths, first_seg, local_count, 0)
    weights = jnp.concatenate(
        [
            lin_qkv[:, 0],
            lin_qkv[:, 1],
            lin_qkv[:, 2],
            lin_gates[:, 0],
            lin_gates[:, 1],
            jnp.zeros((model_width, 128 - 2 * local_heads), bf16),
        ],
        axis=1,
    )
    kv_head = tensor_idx // (tensor_count // KV_HEADS)
    own_kv = jnp.concatenate(
        [
            lax.dynamic_slice_in_dim(att_kv[:, c], kv_head * att_dim, att_dim, 1)
            for c in range(2)
        ],
        axis=1,
    )
    seg_ids = jnp.arange(segment_count)
    parent_map = ((parents[:, None] == seg_ids[None, :]) & (seg_ids[:, None] > 0)).astype(f32)
    seen = (ancestor_table(parent_map) > 0.5) | (seg_ids[:, None] == seg_ids[None, :])
    seen = lax.dynamic_slice_in_dim(seen, first_seg, local_count, 0)
    places = jnp.arange(SEG)
    key_valid = places[None, :] < lengths[:, None]
    bias = jnp.where(seen[:, :, None] & key_valid[None], 0.0, -1e30)
    bias = bias.astype(f32).reshape(local_count, segment_count * SEG)
    valid = (places[None, :] < own_lengths[:, None]).astype(f32).reshape(local_rows, 1)
    o1, q2, amap, bmap = delta_terms(tokens, weights, own_lengths, decay_rate, head_dim)
    lin_mixed, normed = mix_rows(
        parents, amap, bmap, o1, q2, full_out, tokens, norm_gain[None, :]
    )
    return lin_mixed, attend(normed, att_q, own_kv, bias, valid)


def attend_kernel(
    branches, tensors, normed_ref, q_w_ref, kv_w_ref, bias_ref, valid_ref, out_ref,
    kv, queries, accum, top, sums, far_send, far_recv, pass_send, pass_recv,
):
    me_b = lax.axis_index("branch")
    me_t = lax.axis_index("tensor")
    core = lax.rem(me_t, 2)
    partner = me_t + 1 - 2 * core
    rows = normed_ref.shape[0]
    count = rows // SEG
    half = rows // 2
    heads = q_w_ref.shape[1] // ATT_DIM

    barrier = pltpu.get_barrier_semaphore()
    for d in range(1, branches):
        pl.semaphore_signal(
            barrier, inc=1, device_id={"branch": lax.rem(me_b + d, branches)}, device_id_type=MESH
        )
    pl.semaphore_signal(barrier, inc=1, device_id={"tensor": partner}, device_id_type=MESH)

    def keys_of(branch, part):
        return pl.ds(pl.multiple_of(branch * rows + part * half, half), half)

    def far_copy(peer, source):
        return pltpu.make_async_remote_copy(
            src_ref=kv.at[keys_of(source, core)], dst_ref=kv.at[keys_of(source, core)],
            send_sem=far_send.at[peer], recv_sem=far_recv.at[source],
            device_id={"branch": peer}, device_id_type=MESH,
        )

    def pass_copy(source, part):
        return pltpu.make_async_remote_copy(
            src_ref=kv.at[keys_of(source, part)], dst_ref=kv.at[keys_of(source, part)],
            send_sem=pass_send.at[source], recv_sem=pass_recv.at[source],
            device_id={"tensor": partner}, device_id_type=MESH,
        )

    def project_half(part):
        at = pl.ds(pl.multiple_of(part * half, half), half)
        kv[keys_of(me_b, part), :] = dot1(normed_ref[at, :], kv_w_ref[...]).astype(bf16)

    project_half(core)
    pl.semaphore_wait(barrier, branches)
    for peer in range(1, branches):
        @pl.when(me_b < peer)
        def _():
            far_copy(peer, me_b).start()
    project_half(1 - core)

    scale = 1.0 / math.sqrt(ATT_DIM)

    def query_rows(j):
        return pl.ds(pl.multiple_of(j * SEG, SEG), SEG)

    def project(j, carry):
        part = dot1(normed_ref[query_rows(j), :], q_w_ref[...]).astype(bf16) * scale
        for h in range(heads):
            queries[j, h * SEG : (h + 1) * SEG, :] = (
                part[:, h * ATT_DIM : (h + 1) * ATT_DIM].astype(bf16)
            )
        return carry

    lax.fori_loop(0, count, project, 0)

    causal_row = lax.broadcasted_iota(jnp.int32, (heads * SEG, SEG), 0) % SEG
    causal_col = lax.broadcasted_iota(jnp.int32, (heads * SEG, SEG), 1)
    causal = jnp.where(causal_col <= causal_row, 0.0, -1e30)
    for j in range(count):
        seen = j + 1
        span = pl.ds(pl.multiple_of(me_b * rows, SEG), seen * SEG)
        scores = dot1(queries[j], kv[span, :ATT_DIM], NT) + bias_ref[j : j + 1, span]
        tail = scores[:, j * SEG :] + causal
        scores = tail if j == 0 else jnp.concatenate([scores[:, : j * SEG], tail], axis=1)
        best = jnp.max(scores, axis=1, keepdims=True)
        numer = jnp.exp(scores - best)
        top[j] = jnp.broadcast_to(best, top.shape[1:])
        sums[j] = jnp.broadcast_to(jnp.sum(numer, axis=1, keepdims=True), sums.shape[1:])
        accum[j] = dot1(numer.astype(bf16), kv[span, ATT_DIM:])

    def earlier(source, carry):
        far_copy(0, source).wait_recv()
        pass_copy(source, core).start()
        pass_copy(source, 1 - core).wait_recv()
        span = pl.ds(pl.multiple_of(source * rows, SEG), rows)

        def one(j, inner):
            scores = dot1(queries[j], kv[span, :ATT_DIM], NT) + bias_ref[pl.ds(j, 1), span]
            old = top[j][:, :1]
            best = jnp.maximum(old, jnp.max(scores, axis=1, keepdims=True))
            numer = jnp.exp(scores - best)
            keep = jnp.exp(old - best)
            top[j] = jnp.broadcast_to(best, top.shape[1:])
            sums[j] = sums[j] * keep + jnp.sum(numer, axis=1, keepdims=True)
            accum[j] = accum[j] * keep + dot1(numer.astype(bf16), kv[span, ATT_DIM:])
            return inner

        lax.fori_loop(0, count, one, 0)
        return carry

    lax.fori_loop(0, me_b, earlier, 0)

    def store(j, carry):
        result = accum[j] / sums[j][:, :1]
        keep = valid_ref[query_rows(j), :] > 0
        for h in range(heads):
            out_ref[query_rows(j), h * ATT_DIM : (h + 1) * ATT_DIM] = jnp.where(
                keep, result[h * SEG : (h + 1) * SEG], 0.0
            ).astype(bf16)
        return carry

    lax.fori_loop(0, count, store, 0)

    for peer in range(1, branches):
        @pl.when(me_b < peer)
        def _():
            far_copy(peer, me_b).wait_send()

    def finish(source, carry):
        pass_copy(source, core).wait_send()
        return carry

    lax.fori_loop(0, me_b, finish, 0)


def attend(normed, att_q, own_kv, bias, valid):
    branches, tensors = lax.axis_size("branch"), lax.axis_size("tensor")
    rows = normed.shape[0]
    count = rows // SEG
    heads = att_q.shape[1] // ATT_DIM
    vmem = pl.BlockSpec(memory_space=pltpu.VMEM)
    dma = pltpu.SemaphoreType.DMA
    return pl.pallas_call(
        functools.partial(attend_kernel, branches, tensors),
        in_specs=[vmem] * 5,
        out_specs=vmem,
        out_shape=jax.ShapeDtypeStruct((rows, att_q.shape[1]), bf16),
        scratch_shapes=[
            pltpu.VMEM((branches * rows, 2 * ATT_DIM), bf16),
            pltpu.VMEM((count, heads * SEG, ATT_DIM), bf16),
            pltpu.VMEM((count, heads * SEG, ATT_DIM), f32),
            pltpu.VMEM((count, heads * SEG, 128), f32),
            pltpu.VMEM((count, heads * SEG, 128), f32),
            dma((branches,)),
            dma((branches,)),
            dma((branches,)),
            dma((branches,)),
        ],
        compiler_params=pltpu.CompilerParams(
            collective_id=1, has_side_effects=True, vmem_limit_bytes=56 * MIB
        ),
    )(normed, att_q, own_kv, bias, valid)


def solution(mesh):
    placed = (
        P(("rollout", "branch"), None),
        P("rollout"),
        P("rollout"),
        P(None, None, "tensor"),
        P(None, None, "tensor"),
        P("tensor"),
        P("tensor", None),
        P(),
        P(None, "tensor"),
        P(),
    )
    return jax.shard_map(
        on_device,
        mesh=mesh,
        in_specs=placed,
        out_specs=(P(("rollout", "branch", "tensor"), None), P(("rollout", "branch"), "tensor")),
        check_vma=False,
    )
```

```python
import functools
import math

import jax
import jax.numpy as jnp
from jax import lax
from jax.experimental import pallas as pl
from jax.experimental.pallas import tpu as pltpu
from jax.sharding import PartitionSpec as P

KV_HEADS = 2
ATT_DIM = 256
SEG = 256
MIB = 1024 * 1024

f32 = jnp.float32
bf16 = jnp.bfloat16
highest = lax.Precision.HIGHEST
MESH = pl.DeviceIdType.MESH

NN = (((1,), (0,)), ((), ()))
NT = (((1,), (1,)), ((), ()))
TN = (((0,), (0,)), ((), ()))


def dot1(a, b, dims=NN):
    return lax.dot_general(a, b, dims, preferred_element_type=f32)


def split(x):
    high = x.astype(bf16)
    return high, (x - high.astype(f32)).astype(bf16)


def dot3(a, b, dims=NN):
    (ah, al), (bh, bl) = a, b
    ax, bx = dims[0][0][0], dims[0][1][0]
    left = jnp.concatenate([ah, ah, al], axis=ax)
    right = jnp.concatenate([bh, bl, bh], axis=bx)
    return dot1(left, right, dims)


def unit_rows(matrix):
    return matrix * lax.rsqrt(jnp.sum(matrix * matrix, axis=-1, keepdims=True) + 1e-06)


def delta_kernel(
    heads, dim, per, lens_ref, rate_ref, tok_ref, w_ref, gate_ref, o1_ref, q2_ref, a_ref, b_ref
):
    toks = tok_ref[...]
    projected = [dot1(toks, w_ref[c]) for c in range(3)]
    gates_all = dot1(toks, gate_ref[...], NT)
    half = SEG // 2
    rows = lax.broadcasted_iota(jnp.int32, (SEG, SEG), 0)
    cols = lax.broadcasted_iota(jnp.int32, (SEG, SEG), 1)
    strict = rows > cols
    inclusive = rows >= cols
    tril = inclusive.astype(f32)
    hrows = lax.broadcasted_iota(jnp.int32, (half, half), 0)
    hcols = lax.broadcasted_iota(jnp.int32, (half, half), 1)
    places = lax.broadcasted_iota(jnp.int32, (SEG, 1), 0)
    eye = (hrows == hcols).astype(f32)
    parts = []
    for g in range(per):
        valid = places < lens_ref[pl.program_id(0) * per + g]
        queries, keys, values = (p[g * SEG : (g + 1) * SEG] for p in projected)
        gates = gates_all[g * SEG : (g + 1) * SEG]
        for h in range(heads):
            at = slice(h * dim, (h + 1) * dim)
            q = unit_rows(queries[:, at]) / math.sqrt(dim)
            k = unit_rows(keys[:, at])
            v = values[:, at]
            g0 = gates[:, h : h + 1]
            g1 = gates[:, heads + h : heads + h + 1]
            beta = jnp.where(valid, 1.0 / (1.0 + jnp.exp(-g1)), 0.0)
            soft = jnp.maximum(g0, 0.0) + jnp.log1p(jnp.exp(-jnp.abs(g0)))
            step = jnp.where(valid, -rate_ref[h] * soft, 0.0)
            total = lax.dot_general(
                tril, jnp.broadcast_to(step, (SEG, dim)), NN, precision=highest,
                preferred_element_type=f32,
            )
            col = total[:, :1]
            row = total.T[:1, :]
            decay = jnp.exp(jnp.where(inclusive, col - row, 0.0))
            ks = split(k)
            key_key = dot3(ks, ks, NT)
            query_key = dot3(split(q), ks, NT)
            lower = jnp.where(strict, beta * decay * key_key, 0.0)
            mixing = jnp.where(inclusive, decay * query_key, 0.0)
            grown = jnp.exp(col)
            right = jnp.concatenate([beta * v, (beta * grown) * k], axis=1)
            last = total[SEG - 1 :, :]
            carried = jnp.exp(last - total) * k
            parts.append([lower, mixing, right, carried, grown * q, jnp.exp(last), valid])
    lowers = [
        p[0][c * half : (c + 1) * half, c * half : (c + 1) * half] for p in parts for c in range(2)
    ]
    inverses = [eye - jnp.where(hrows // 2 == hcols // 2, x, 0.0) for x in lowers]
    size = 2
    while size < half:
        pair = (hrows // (2 * size) == hcols // (2 * size)) & (hrows // size != hcols // size)
        halves = [split(x) for x in inverses]
        inner = [
            split(dot3(split(jnp.where(pair, x, 0.0)), y)) for x, y in zip(lowers, halves)
        ]
        inverses = [x - dot3(xs, y) for x, xs, y in zip(inverses, halves, inner)]
        size *= 2
    inverses = [split(x) for x in inverses]
    for g in range(per):
        for h in range(heads):
            n = g * heads + h
            lower, mixing, right, carried, queries, overall, valid = parts[n]
            upper = dot3(inverses[2 * n], split(right[:half]))
            rest = right[half:] - dot3(split(lower[half:, :half]), split(upper))
            bottom = dot3(inverses[2 * n + 1], split(rest))
            solved = split(jnp.concatenate([upper, bottom], axis=0))
            out = dot3(split(mixing), solved)
            ends = dot3(split(carried), solved, TN)
            at = slice(g * SEG, (g + 1) * SEG)
            o1_ref[at, h * dim : (h + 1) * dim] = jnp.where(valid, out[:, :dim], 0.0)
            q2_ref[at, h * dim : (h + 1) * dim] = jnp.where(valid, queries - out[:, dim:], 0.0)
            b_ref[g, h] = ends[:, :dim]
            a_ref[g, h] = overall * eye - ends[:, dim:]


def delta_terms(tokens, weights, gates, own_lengths, decay_rate, dim):
    heads = decay_rate.shape[0]
    rows, model = tokens.shape
    count = rows // SEG
    per = 2 - count % 2
    maps = jax.ShapeDtypeStruct((count, heads, dim, dim), f32)
    flat = jax.ShapeDtypeStruct((rows, heads * dim), f32)
    smem = pl.BlockSpec(memory_space=pltpu.SMEM)
    return pl.pallas_call(
        functools.partial(delta_kernel, heads, dim, per),
        grid=(count // per,),
        in_specs=[
            smem,
            smem,
            pl.BlockSpec((per * SEG, model), lambda s: (s, 0)),
            pl.BlockSpec(weights.shape, lambda s: (0, 0, 0)),
            pl.BlockSpec(gates.shape, lambda s: (0, 0)),
        ],
        out_specs=[
            pl.BlockSpec((per * SEG, heads * dim), lambda s: (s, 0)),
            pl.BlockSpec((per * SEG, heads * dim), lambda s: (s, 0)),
            pl.BlockSpec((per, heads, dim, dim), lambda s: (s, 0, 0, 0)),
            pl.BlockSpec((per, heads, dim, dim), lambda s: (s, 0, 0, 0)),
        ],
        out_shape=[flat, flat, maps, maps],
        compiler_params=pltpu.CompilerParams(vmem_limit_bytes=48 * MIB),
    )(own_lengths, decay_rate, tokens, weights, gates)


def mix_kernel(
    branches, tensors, parents_ref, a_ref, b_ref, o1_ref, q2_ref, lin_out_ref, tok_ref, gain_ref,
    mixed_ref, normed_ref,
    ends, ends16, starts, lin, total, end_send, end_recv, near_send, near_recv, far_send, far_recv,
    pass_send, pass_recv,
):
    me_b = lax.axis_index("branch")
    me_t = lax.axis_index("tensor")
    count, heads, dim, _ = a_ref.shape
    model = tok_ref.shape[1]
    chunk = mixed_ref.shape[0]
    chunks = lin.shape[1] // chunk
    width = heads * dim
    chips = tensors // 2
    chip, core = me_t // 2, me_t % 2
    partner = chip * 2 + (1 - core)
    ends[...] = jnp.zeros_like(ends)

    def far_of(f):
        return lax.rem(chip + 1 + f, chips)

    barrier = pltpu.get_barrier_semaphore()
    for d in range(1, branches):
        pl.semaphore_signal(
            barrier, inc=1, device_id={"branch": lax.rem(me_b + d, branches)}, device_id_type=MESH
        )
    pl.semaphore_signal(barrier, inc=1, device_id={"tensor": partner}, device_id_type=MESH)
    for f in range(chips - 1):
        pl.semaphore_signal(
            barrier, inc=1, device_id={"tensor": far_of(f) * 2 + core}, device_id_type=MESH
        )
    pl.semaphore_wait(barrier, branches - 1 + chips)

    first = me_b * count

    def end_copy(j, peer):
        return pltpu.make_async_remote_copy(
            src_ref=ends16.at[first + j], dst_ref=ends16.at[first + j],
            send_sem=end_send.at[j, peer], recv_sem=end_recv.at[first + j],
            device_id={"branch": peer}, device_id_type=MESH,
        )

    def take_end(s, carry):
        pltpu.make_async_remote_copy(
            src_ref=ends16.at[s], dst_ref=ends16.at[s],
            send_sem=end_send.at[0, 0], recv_sem=end_recv.at[s],
            device_id={"branch": lax.rem(me_b + 1, branches)}, device_id_type=MESH,
        ).wait_recv()
        ends[s] = ends16[s].astype(f32)
        return carry

    lax.fori_loop(0, first, take_end, 0)

    def advance(j, carry):
        s = first + j
        start = ends[parents_ref[s]]
        start = jnp.where(s > 0, start, jnp.zeros_like(start))
        starts[j] = start
        for h in range(heads):
            done = dot3(split(a_ref[j, h]), split(start[h])) + b_ref[j, h]
            ends[s, h] = done
            ends16[s, h] = done.astype(bf16)
        for peer in range(1, branches):
            @pl.when(me_b < peer)
            def _():
                end_copy(j, peer).start()
        return carry

    lax.fori_loop(0, count, advance, 0)

    def rows_of(i):
        return pl.ds(pl.multiple_of(i * chunk, chunk), chunk)

    def near_copy(i):
        return pltpu.make_async_remote_copy(
            src_ref=lin.at[me_t, rows_of(i)], dst_ref=lin.at[me_t, rows_of(i)],
            send_sem=near_send.at[i], recv_sem=near_recv.at[i],
            device_id={"tensor": partner}, device_id_type=MESH,
        )

    def far_copy(i, f):
        return pltpu.make_async_remote_copy(
            src_ref=lin.at[me_t, rows_of(i)], dst_ref=lin.at[me_t, rows_of(i)],
            send_sem=far_send.at[i, f], recv_sem=far_recv.at[i, f],
            device_id={"tensor": far_of(f) * 2 + core}, device_id_type=MESH,
        )

    def pass_copy(i, f):
        source = lax.rem(chip + chips - 1 - f, chips) * 2 + core
        return pltpu.make_async_remote_copy(
            src_ref=lin.at[source, rows_of(i)], dst_ref=lin.at[source, rows_of(i)],
            send_sem=pass_send.at[i, f], recv_sem=pass_recv.at[i, f],
            device_id={"tensor": partner}, device_id_type=MESH,
        )

    def produce(i, carry):
        j = (i * chunk) // SEG
        for h in range(heads):
            cols = slice(h * dim, (h + 1) * dim)
            out = o1_ref[rows_of(i), cols] + dot3(
                split(q2_ref[rows_of(i), cols]), split(starts[j, h])
            )
            lin[me_t, rows_of(i), cols] = out.astype(bf16)
        for f in range(chips - 1):
            far_copy(i, f).start()
        near_copy(i).start()
        return carry

    lax.fori_loop(0, chunks, produce, 0)

    def forward(i, carry):
        for f in range(chips - 1):
            far_copy(i, f).wait_recv()
            pass_copy(i, f).start()
        return carry

    tile = 512

    def mix(i, carry):
        forward(i, 0)
        near_copy(i).wait_recv()
        for f in range(chips - 1):
            pass_copy(i, f).wait_recv()

        def column(n, squares):
            cols = pl.ds(pl.multiple_of(n * tile, tile), tile)
            part = tok_ref[rows_of(i), cols].astype(f32)
            for t in range(tensors):
                part = part + dot1(
                    lin[t, rows_of(i), :], lin_out_ref[t * width : (t + 1) * width, cols]
                )
            total[:, cols] = part
            return squares + jnp.sum(part * part, axis=1, keepdims=True)

        squares = lax.fori_loop(0, model // tile, column, jnp.zeros((chunk, 1), f32))
        scale = lax.rsqrt(squares / model + 1e-06)
        normed_ref[rows_of(i), :] = (total[...] * scale * gain_ref[...]).astype(bf16)

        @pl.when(i == me_t)
        def _():
            mixed_ref[...] = total[...].astype(bf16)

        return carry

    lax.fori_loop(0, chunks, mix, 0)

    def finish(i, carry):
        near_copy(i).wait_send()
        for f in range(chips - 1):
            far_copy(i, f).wait_send()
            pass_copy(i, f).wait_send()
        return carry

    lax.fori_loop(0, chunks, finish, 0)

    def finish_ends(j, carry):
        for peer in range(1, branches):
            @pl.when(me_b < peer)
            def _():
                end_copy(j, peer).wait_send()
        return carry

    lax.fori_loop(0, count, finish_ends, 0)


def mix_rows(parents, amap, bmap, o1, q2, lin_out, tokens, gain):
    branches, tensors = lax.axis_size("branch"), lax.axis_size("tensor")
    count, heads, dim, _ = amap.shape
    rows, model = tokens.shape
    chunk = rows // tensors
    chunks = tensors
    segments = branches * count
    fars = max(tensors // 2 - 1, 1)
    vmem = pl.BlockSpec(memory_space=pltpu.VMEM)
    dma = pltpu.SemaphoreType.DMA
    return pl.pallas_call(
        functools.partial(mix_kernel, branches, tensors),
        in_specs=[pl.BlockSpec(memory_space=pltpu.SMEM)] + [vmem] * 7,
        out_specs=[vmem, vmem],
        out_shape=[
            jax.ShapeDtypeStruct((chunk, model), bf16),
            jax.ShapeDtypeStruct((rows, model), bf16),
        ],
        scratch_shapes=[
            pltpu.VMEM((segments, heads, dim, dim), f32),
            pltpu.VMEM((segments, heads, dim, dim), bf16),
            pltpu.VMEM((count, heads, dim, dim), f32),
            pltpu.VMEM((tensors, rows, heads * dim), bf16),
            pltpu.VMEM((chunk, model), f32),
            dma((count, branches)),
            dma((segments,)),
            dma((chunks,)),
            dma((chunks,)),
            dma((chunks, fars)),
            dma((chunks, fars)),
            dma((chunks, fars)),
            dma((chunks, fars)),
        ],
        compiler_params=pltpu.CompilerParams(
            collective_id=0, has_side_effects=True, vmem_limit_bytes=56 * MIB
        ),
    )(parents, amap, bmap, o1, q2, lin_out, tokens, gain)


def on_device(
    tokens, parents, lengths, lin_qkv, lin_gates, decay_rate, lin_out, norm_gain, att_q, att_kv
):
    branch_idx = lax.axis_index("branch")
    tensor_count = lax.axis_size("tensor")
    tensor_idx = lax.axis_index("tensor")
    local_rows, model_width = tokens.shape
    local_count = local_rows // SEG
    segment_count = lax.axis_size("branch") * local_count
    local_heads = decay_rate.shape[0]
    head_dim = lin_qkv.shape[2] // local_heads
    att_dim = ATT_DIM
    first_seg = branch_idx * local_count
    full_out = lax.all_gather(lin_out, "tensor", axis=0, tiled=True)
    own_lengths = lax.dynamic_slice_in_dim(lengths, first_seg, local_count, 0)
    weights = jnp.transpose(lin_qkv, (1, 0, 2))
    gates = jnp.transpose(lin_gates, (1, 2, 0)).reshape(2 * local_heads, model_width)
    kv_head = tensor_idx // (tensor_count // KV_HEADS)
    own_kv = lax.dynamic_slice_in_dim(att_kv, kv_head * att_dim, att_dim, 2)
    own_kv = own_kv.reshape(model_width, 2 * att_dim)
    seg_ids = jnp.arange(segment_count)
    parent_map = ((parents[:, None] == seg_ids[None, :]) & (seg_ids[:, None] > 0)).astype(f32)
    reach = parent_map + jnp.eye(segment_count, dtype=f32)
    for _ in range((segment_count - 1).bit_length()):
        reach = (jnp.dot(reach, reach, precision=highest) > 0.5).astype(f32)
    seen = reach > 0.5
    seen = lax.dynamic_slice_in_dim(seen, first_seg, local_count, 0)
    places = jnp.arange(SEG)
    key_valid = places[None, :] < lengths[:, None]
    bias = jnp.where(seen[:, :, None] & key_valid[None], 0.0, -1e30)
    bias = bias.astype(f32).reshape(local_count, segment_count * SEG)
    o1, q2, amap, bmap = delta_terms(tokens, weights, gates, own_lengths, decay_rate, head_dim)
    lin_mixed, normed = mix_rows(
        parents, amap, bmap, o1, q2, full_out, tokens, norm_gain[None, :]
    )
    return lin_mixed, attend(normed, att_q, own_kv, bias, own_lengths)


def attend_kernel(
    branches, tensors, normed_ref, q_w_ref, kv_w_ref, bias_ref, lens_ref, out_ref,
    kv, queries, accum, top, sums, far_send, far_recv, pass_send, pass_recv,
):
    me_b = lax.axis_index("branch")
    me_t = lax.axis_index("tensor")
    core = lax.rem(me_t, 2)
    partner = me_t + 1 - 2 * core
    rows = normed_ref.shape[0]
    count = rows // SEG
    half = rows // 2
    heads = q_w_ref.shape[1] // ATT_DIM

    barrier = pltpu.get_barrier_semaphore()
    for d in range(1, branches):
        pl.semaphore_signal(
            barrier, inc=1, device_id={"branch": lax.rem(me_b + d, branches)}, device_id_type=MESH
        )
    pl.semaphore_signal(barrier, inc=1, device_id={"tensor": partner}, device_id_type=MESH)

    def keys_of(branch, part):
        return pl.ds(pl.multiple_of(branch * rows + part * half, half), half)

    def far_copy(peer, source):
        return pltpu.make_async_remote_copy(
            src_ref=kv.at[keys_of(source, core)], dst_ref=kv.at[keys_of(source, core)],
            send_sem=far_send.at[peer], recv_sem=far_recv.at[source],
            device_id={"branch": peer}, device_id_type=MESH,
        )

    def pass_copy(source, part):
        return pltpu.make_async_remote_copy(
            src_ref=kv.at[keys_of(source, part)], dst_ref=kv.at[keys_of(source, part)],
            send_sem=pass_send.at[source], recv_sem=pass_recv.at[source],
            device_id={"tensor": partner}, device_id_type=MESH,
        )

    def project_half(part):
        at = pl.ds(pl.multiple_of(part * half, half), half)
        kv[keys_of(me_b, part), :] = dot1(normed_ref[at, :], kv_w_ref[...]).astype(bf16)

    project_half(core)
    pl.semaphore_wait(barrier, branches)
    for peer in range(1, branches):
        @pl.when(me_b < peer)
        def _():
            far_copy(peer, me_b).start()
    project_half(1 - core)

    scale = 1.0 / math.sqrt(ATT_DIM)

    def query_rows(j):
        return pl.ds(pl.multiple_of(j * SEG, SEG), SEG)

    def project(j, carry):
        part = dot1(normed_ref[query_rows(j), :], q_w_ref[...]).astype(bf16) * scale
        for h in range(heads):
            queries[j, h * SEG : (h + 1) * SEG, :] = (
                part[:, h * ATT_DIM : (h + 1) * ATT_DIM].astype(bf16)
            )
        return carry

    lax.fori_loop(0, count, project, 0)

    causal_row = lax.broadcasted_iota(jnp.int32, (heads * SEG, SEG), 0) % SEG
    causal_col = lax.broadcasted_iota(jnp.int32, (heads * SEG, SEG), 1)
    causal = jnp.where(causal_col <= causal_row, 0.0, -1e30)
    for j in range(count):
        seen = j + 1
        span = pl.ds(pl.multiple_of(me_b * rows, SEG), seen * SEG)
        scores = dot1(queries[j], kv[span, :ATT_DIM], NT) + bias_ref[j : j + 1, span]
        tail = scores[:, j * SEG :] + causal
        scores = tail if j == 0 else jnp.concatenate([scores[:, : j * SEG], tail], axis=1)
        best = jnp.max(scores, axis=1, keepdims=True)
        numer = jnp.exp(scores - best)
        top[j] = jnp.broadcast_to(best, top.shape[1:])
        sums[j] = jnp.broadcast_to(jnp.sum(numer, axis=1, keepdims=True), sums.shape[1:])
        accum[j] = dot1(numer.astype(bf16), kv[span, ATT_DIM:])

    def earlier(source, carry):
        far_copy(0, source).wait_recv()
        pass_copy(source, core).start()
        pass_copy(source, 1 - core).wait_recv()
        span = pl.ds(pl.multiple_of(source * rows, SEG), rows)

        def one(j, inner):
            scores = dot1(queries[j], kv[span, :ATT_DIM], NT) + bias_ref[pl.ds(j, 1), span]
            old = top[j][:, :1]
            best = jnp.maximum(old, jnp.max(scores, axis=1, keepdims=True))
            numer = jnp.exp(scores - best)
            keep = jnp.exp(old - best)
            top[j] = jnp.broadcast_to(best, top.shape[1:])
            sums[j] = sums[j] * keep + jnp.sum(numer, axis=1, keepdims=True)
            accum[j] = accum[j] * keep + dot1(numer.astype(bf16), kv[span, ATT_DIM:])
            return inner

        lax.fori_loop(0, count, one, 0)
        return carry

    lax.fori_loop(0, me_b, earlier, 0)

    def store(j, carry):
        result = accum[j] / sums[j][:, :1]
        keep = lax.broadcasted_iota(jnp.int32, (SEG, 1), 0) < lens_ref[j]
        for h in range(heads):
            out_ref[query_rows(j), h * ATT_DIM : (h + 1) * ATT_DIM] = jnp.where(
                keep, result[h * SEG : (h + 1) * SEG], 0.0
            ).astype(bf16)
        return carry

    lax.fori_loop(0, count, store, 0)

    for peer in range(1, branches):
        @pl.when(me_b < peer)
        def _():
            far_copy(peer, me_b).wait_send()

    def finish(source, carry):
        pass_copy(source, core).wait_send()
        return carry

    lax.fori_loop(0, me_b, finish, 0)


def attend(normed, att_q, own_kv, bias, own_lengths):
    branches, tensors = lax.axis_size("branch"), lax.axis_size("tensor")
    rows = normed.shape[0]
    count = rows // SEG
    heads = att_q.shape[1] // ATT_DIM
    vmem = pl.BlockSpec(memory_space=pltpu.VMEM)
    dma = pltpu.SemaphoreType.DMA
    return pl.pallas_call(
        functools.partial(attend_kernel, branches, tensors),
        in_specs=[vmem] * 4 + [pl.BlockSpec(memory_space=pltpu.SMEM)],
        out_specs=vmem,
        out_shape=jax.ShapeDtypeStruct((rows, att_q.shape[1]), bf16),
        scratch_shapes=[
            pltpu.VMEM((branches * rows, 2 * ATT_DIM), bf16),
            pltpu.VMEM((count, heads * SEG, ATT_DIM), bf16),
            pltpu.VMEM((count, heads * SEG, ATT_DIM), f32),
            pltpu.VMEM((count, heads * SEG, 128), f32),
            pltpu.VMEM((count, heads * SEG, 128), f32),
            dma((branches,)),
            dma((branches,)),
            dma((branches,)),
            dma((branches,)),
        ],
        compiler_params=pltpu.CompilerParams(
            collective_id=1, has_side_effects=True, vmem_limit_bytes=56 * MIB
        ),
    )(normed, att_q, own_kv, bias, own_lengths)


def solution(mesh):
    placed = (
        P(("rollout", "branch"), None),
        P("rollout"),
        P("rollout"),
        P(None, None, "tensor"),
        P(None, None, "tensor"),
        P("tensor"),
        P("tensor", None),
        P(),
        P(None, "tensor"),
        P(),
    )
    return jax.shard_map(
        on_device,
        mesh=mesh,
        in_specs=placed,
        out_specs=(P(("rollout", "branch", "tensor"), None), P(("rollout", "branch"), "tensor")),
        check_vma=False,
    )
```

```python
import functools
import math

import jax
import jax.numpy as jnp
from jax import lax
from jax.experimental import pallas as pl
from jax.experimental.pallas import tpu as pltpu
from jax.sharding import PartitionSpec as P

KV_HEADS = 2
ATT_DIM = 256
SEG = 256
MIB = 1024 * 1024

f32 = jnp.float32
bf16 = jnp.bfloat16
highest = lax.Precision.HIGHEST
MESH = pl.DeviceIdType.MESH

NN = (((1,), (0,)), ((), ()))
NT = (((1,), (1,)), ((), ()))
TN = (((0,), (0,)), ((), ()))


def dot1(a, b, dims=NN):
    return lax.dot_general(a, b, dims, preferred_element_type=f32)


def split(x):
    high = x.astype(bf16)
    return high, (x - high.astype(f32)).astype(bf16)


def dot3(a, b, dims=NN):
    (ah, al), (bh, bl) = a, b
    ax, bx = dims[0][0][0], dims[0][1][0]
    left = jnp.concatenate([ah, ah, al], axis=ax)
    right = jnp.concatenate([bh, bl, bh], axis=bx)
    return dot1(left, right, dims)


def unit_rows(matrix):
    return matrix * lax.rsqrt(jnp.sum(matrix * matrix, axis=-1, keepdims=True) + 1e-06)


def delta_kernel(
    heads, dim, per, lens_ref, rate_ref, tok_ref, w_ref, gate_ref, o1_ref, q2_ref, a_ref, b_ref
):
    toks = tok_ref[...]
    projected = [dot1(toks, w_ref[c]) for c in range(3)]
    gates_all = dot1(toks, gate_ref[...], NT)
    half = SEG // 2
    rows = lax.broadcasted_iota(jnp.int32, (SEG, SEG), 0)
    cols = lax.broadcasted_iota(jnp.int32, (SEG, SEG), 1)
    strict = rows > cols
    inclusive = rows >= cols
    tril = inclusive.astype(f32)
    hrows = lax.broadcasted_iota(jnp.int32, (half, half), 0)
    hcols = lax.broadcasted_iota(jnp.int32, (half, half), 1)
    places = lax.broadcasted_iota(jnp.int32, (SEG, 1), 0)
    eye = (hrows == hcols).astype(f32)
    parts = []
    for g in range(per):
        valid = places < lens_ref[pl.program_id(0) * per + g]
        queries, keys, values = (p[g * SEG : (g + 1) * SEG] for p in projected)
        gates = gates_all[g * SEG : (g + 1) * SEG]
        for h in range(heads):
            at = slice(h * dim, (h + 1) * dim)
            q = unit_rows(queries[:, at]) / math.sqrt(dim)
            k = unit_rows(keys[:, at])
            v = values[:, at]
            g0 = gates[:, h : h + 1]
            g1 = gates[:, heads + h : heads + h + 1]
            beta = jnp.where(valid, 1.0 / (1.0 + jnp.exp(-g1)), 0.0)
            soft = jnp.maximum(g0, 0.0) + jnp.log1p(jnp.exp(-jnp.abs(g0)))
            step = jnp.where(valid, -rate_ref[h] * soft, 0.0)
            total = lax.dot_general(
                tril, jnp.broadcast_to(step, (SEG, dim)), NN, precision=highest,
                preferred_element_type=f32,
            )
            col = total[:, :1]
            row = total.T[:1, :]
            decay = jnp.exp(jnp.where(inclusive, col - row, 0.0))
            ks = split(k)
            key_key = dot3(ks, ks, NT)
            query_key = dot3(split(q), ks, NT)
            lower = jnp.where(strict, beta * decay * key_key, 0.0)
            mixing = jnp.where(inclusive, decay * query_key, 0.0)
            grown = jnp.exp(col)
            right = jnp.concatenate([beta * v, (beta * grown) * k], axis=1)
            last = total[SEG - 1 :, :]
            carried = jnp.exp(last - total) * k
            parts.append([lower, mixing, right, carried, grown * q, jnp.exp(last), valid])
    lowers = [
        p[0][c * half : (c + 1) * half, c * half : (c + 1) * half] for p in parts for c in range(2)
    ]
    inverses = [eye - jnp.where(hrows // 2 == hcols // 2, x, 0.0) for x in lowers]
    size = 2
    while size < half:
        pair = (hrows // (2 * size) == hcols // (2 * size)) & (hrows // size != hcols // size)
        halves = [split(x) for x in inverses]
        inner = [
            split(dot3(split(jnp.where(pair, x, 0.0)), y)) for x, y in zip(lowers, halves)
        ]
        inverses = [x - dot3(xs, y) for x, xs, y in zip(inverses, halves, inner)]
        size *= 2
    inverses = [split(x) for x in inverses]
    for g in range(per):
        for h in range(heads):
            n = g * heads + h
            lower, mixing, right, carried, queries, overall, valid = parts[n]
            upper = dot3(inverses[2 * n], split(right[:half]))
            rest = right[half:] - dot3(split(lower[half:, :half]), split(upper))
            bottom = dot3(inverses[2 * n + 1], split(rest))
            solved = split(jnp.concatenate([upper, bottom], axis=0))
            out = dot3(split(mixing), solved)
            ends = dot3(split(carried), solved, TN)
            at = slice(g * SEG, (g + 1) * SEG)
            o1_ref[at, h * dim : (h + 1) * dim] = jnp.where(valid, out[:, :dim], 0.0)
            q2_ref[at, h * dim : (h + 1) * dim] = jnp.where(valid, queries - out[:, dim:], 0.0)
            b_ref[g, h] = ends[:, :dim]
            a_ref[g, h] = overall * eye - ends[:, dim:]


def delta_terms(tokens, weights, gates, own_lengths, decay_rate, dim):
    heads = decay_rate.shape[0]
    rows, model = tokens.shape
    count = rows // SEG
    per = 2 - count % 2
    maps = jax.ShapeDtypeStruct((count, heads, dim, dim), f32)
    flat = jax.ShapeDtypeStruct((rows, heads * dim), f32)
    smem = pl.BlockSpec(memory_space=pltpu.SMEM)
    return pl.pallas_call(
        functools.partial(delta_kernel, heads, dim, per),
        grid=(count // per,),
        in_specs=[
            smem,
            smem,
            pl.BlockSpec((per * SEG, model), lambda s: (s, 0)),
            pl.BlockSpec(weights.shape, lambda s: (0, 0, 0)),
            pl.BlockSpec(gates.shape, lambda s: (0, 0)),
        ],
        out_specs=[
            pl.BlockSpec((per * SEG, heads * dim), lambda s: (s, 0)),
            pl.BlockSpec((per * SEG, heads * dim), lambda s: (s, 0)),
            pl.BlockSpec((per, heads, dim, dim), lambda s: (s, 0, 0, 0)),
            pl.BlockSpec((per, heads, dim, dim), lambda s: (s, 0, 0, 0)),
        ],
        out_shape=[flat, flat, maps, maps],
        compiler_params=pltpu.CompilerParams(vmem_limit_bytes=36 * MIB),
    )(own_lengths, decay_rate, tokens, weights, gates)


def mix_kernel(
    branches, tensors, parents_ref, a_ref, b_ref, o1_ref, q2_ref, lin_out_ref, tok_ref, gain_ref,
    mixed_ref, normed_ref,
    ends, ends16, starts, lin, total, end_send, end_recv, near_send, near_recv, far_send, far_recv,
    pass_send, pass_recv,
):
    me_b = lax.axis_index("branch")
    me_t = lax.axis_index("tensor")
    count, heads, dim, _ = a_ref.shape
    model = tok_ref.shape[1]
    chunk = mixed_ref.shape[0]
    chunks = lin.shape[1] // chunk
    width = heads * dim
    chips = tensors // 2
    chip, core = me_t // 2, me_t % 2
    partner = chip * 2 + (1 - core)
    ends[...] = jnp.zeros_like(ends)

    def far_of(f):
        return lax.rem(chip + 1 + f, chips)

    barrier = pltpu.get_barrier_semaphore()
    for d in range(1, branches):
        pl.semaphore_signal(
            barrier, inc=1, device_id={"branch": lax.rem(me_b + d, branches)}, device_id_type=MESH
        )
    pl.semaphore_signal(barrier, inc=1, device_id={"tensor": partner}, device_id_type=MESH)
    for f in range(chips - 1):
        pl.semaphore_signal(
            barrier, inc=1, device_id={"tensor": far_of(f) * 2 + core}, device_id_type=MESH
        )
    pl.semaphore_wait(barrier, branches - 1 + chips)

    first = me_b * count

    def end_copy(j, peer):
        return pltpu.make_async_remote_copy(
            src_ref=ends16.at[first + j], dst_ref=ends16.at[first + j],
            send_sem=end_send.at[j, peer], recv_sem=end_recv.at[first + j],
            device_id={"branch": peer}, device_id_type=MESH,
        )

    def take_end(s, carry):
        pltpu.make_async_remote_copy(
            src_ref=ends16.at[s], dst_ref=ends16.at[s],
            send_sem=end_send.at[0, 0], recv_sem=end_recv.at[s],
            device_id={"branch": lax.rem(me_b + 1, branches)}, device_id_type=MESH,
        ).wait_recv()
        ends[s] = ends16[s].astype(f32)
        return carry

    lax.fori_loop(0, first, take_end, 0)

    def advance(j, carry):
        s = first + j
        start = ends[parents_ref[s]]
        start = jnp.where(s > 0, start, jnp.zeros_like(start))
        starts[j] = start
        for h in range(heads):
            done = dot3(split(a_ref[j, h]), split(start[h])) + b_ref[j, h]
            ends[s, h] = done
            ends16[s, h] = done.astype(bf16)
        for peer in range(1, branches):
            @pl.when(me_b < peer)
            def _():
                end_copy(j, peer).start()
        return carry

    lax.fori_loop(0, count, advance, 0)

    def rows_of(i):
        return pl.ds(pl.multiple_of(i * chunk, chunk), chunk)

    def near_copy(i):
        return pltpu.make_async_remote_copy(
            src_ref=lin.at[me_t, rows_of(i)], dst_ref=lin.at[me_t, rows_of(i)],
            send_sem=near_send.at[i], recv_sem=near_recv.at[i],
            device_id={"tensor": partner}, device_id_type=MESH,
        )

    def far_copy(i, f):
        return pltpu.make_async_remote_copy(
            src_ref=lin.at[me_t, rows_of(i)], dst_ref=lin.at[me_t, rows_of(i)],
            send_sem=far_send.at[i, f], recv_sem=far_recv.at[i, f],
            device_id={"tensor": far_of(f) * 2 + core}, device_id_type=MESH,
        )

    def pass_copy(i, f):
        source = lax.rem(chip + chips - 1 - f, chips) * 2 + core
        return pltpu.make_async_remote_copy(
            src_ref=lin.at[source, rows_of(i)], dst_ref=lin.at[source, rows_of(i)],
            send_sem=pass_send.at[i, f], recv_sem=pass_recv.at[i, f],
            device_id={"tensor": partner}, device_id_type=MESH,
        )

    def produce(i, carry):
        j = (i * chunk) // SEG
        for h in range(heads):
            cols = slice(h * dim, (h + 1) * dim)
            out = o1_ref[rows_of(i), cols] + dot3(
                split(q2_ref[rows_of(i), cols]), split(starts[j, h])
            )
            lin[me_t, rows_of(i), cols] = out.astype(bf16)
        for f in range(chips - 1):
            far_copy(i, f).start()
        near_copy(i).start()
        return carry

    lax.fori_loop(0, chunks, produce, 0)

    def forward(i, carry):
        for f in range(chips - 1):
            far_copy(i, f).wait_recv()
            pass_copy(i, f).start()
        return carry

    tile = 512

    def mix(i, carry):
        forward(i, 0)
        near_copy(i).wait_recv()
        for f in range(chips - 1):
            pass_copy(i, f).wait_recv()

        def column(n, squares):
            cols = pl.ds(pl.multiple_of(n * tile, tile), tile)
            part = tok_ref[rows_of(i), cols].astype(f32)
            for t in range(tensors):
                part = part + dot1(
                    lin[t, rows_of(i), :], lin_out_ref[t * width : (t + 1) * width, cols]
                )
            total[:, cols] = part
            return squares + jnp.sum(part * part, axis=1, keepdims=True)

        squares = lax.fori_loop(0, model // tile, column, jnp.zeros((chunk, 1), f32))
        scale = lax.rsqrt(squares / model + 1e-06)
        normed_ref[rows_of(i), :] = (total[...] * scale * gain_ref[...]).astype(bf16)

        @pl.when(i == me_t)
        def _():
            mixed_ref[...] = total[...].astype(bf16)

        return carry

    lax.fori_loop(0, chunks, mix, 0)

    def finish(i, carry):
        near_copy(i).wait_send()
        for f in range(chips - 1):
            far_copy(i, f).wait_send()
            pass_copy(i, f).wait_send()
        return carry

    lax.fori_loop(0, chunks, finish, 0)

    def finish_ends(j, carry):
        for peer in range(1, branches):
            @pl.when(me_b < peer)
            def _():
                end_copy(j, peer).wait_send()
        return carry

    lax.fori_loop(0, count, finish_ends, 0)


def mix_rows(parents, amap, bmap, o1, q2, lin_out, tokens, gain):
    branches, tensors = lax.axis_size("branch"), lax.axis_size("tensor")
    count, heads, dim, _ = amap.shape
    rows, model = tokens.shape
    chunk = rows // tensors
    chunks = tensors
    segments = branches * count
    fars = max(tensors // 2 - 1, 1)
    vmem = pl.BlockSpec(memory_space=pltpu.VMEM)
    dma = pltpu.SemaphoreType.DMA
    return pl.pallas_call(
        functools.partial(mix_kernel, branches, tensors),
        in_specs=[pl.BlockSpec(memory_space=pltpu.SMEM)] + [vmem] * 7,
        out_specs=[vmem, vmem],
        out_shape=[
            jax.ShapeDtypeStruct((chunk, model), bf16),
            jax.ShapeDtypeStruct((rows, model), bf16),
        ],
        scratch_shapes=[
            pltpu.VMEM((segments, heads, dim, dim), f32),
            pltpu.VMEM((segments, heads, dim, dim), bf16),
            pltpu.VMEM((count, heads, dim, dim), f32),
            pltpu.VMEM((tensors, rows, heads * dim), bf16),
            pltpu.VMEM((chunk, model), f32),
            dma((count, branches)),
            dma((segments,)),
            dma((chunks,)),
            dma((chunks,)),
            dma((chunks, fars)),
            dma((chunks, fars)),
            dma((chunks, fars)),
            dma((chunks, fars)),
        ],
        compiler_params=pltpu.CompilerParams(
            collective_id=0, has_side_effects=True, vmem_limit_bytes=30 * MIB
        ),
    )(parents, amap, bmap, o1, q2, lin_out, tokens, gain)


def on_device(
    tokens, parents, lengths, lin_qkv, lin_gates, decay_rate, lin_out, norm_gain, att_q, att_kv
):
    branch_idx = lax.axis_index("branch")
    tensor_count = lax.axis_size("tensor")
    tensor_idx = lax.axis_index("tensor")
    local_rows, model_width = tokens.shape
    local_count = local_rows // SEG
    segment_count = lax.axis_size("branch") * local_count
    local_heads = decay_rate.shape[0]
    head_dim = lin_qkv.shape[2] // local_heads
    att_dim = ATT_DIM
    first_seg = branch_idx * local_count
    full_out = lax.all_gather(lin_out, "tensor", axis=0, tiled=True)
    own_lengths = lax.dynamic_slice_in_dim(lengths, first_seg, local_count, 0)
    weights = jnp.transpose(lin_qkv, (1, 0, 2))
    gates = jnp.transpose(lin_gates, (1, 2, 0)).reshape(2 * local_heads, model_width)
    kv_head = tensor_idx // (tensor_count // KV_HEADS)
    own_kv = lax.dynamic_slice_in_dim(att_kv, kv_head * att_dim, att_dim, 2)
    own_kv = own_kv.reshape(model_width, 2 * att_dim)
    seg_ids = jnp.arange(segment_count)
    parent_map = ((parents[:, None] == seg_ids[None, :]) & (seg_ids[:, None] > 0)).astype(f32)
    reach = parent_map + jnp.eye(segment_count, dtype=f32)
    for _ in range((segment_count - 1).bit_length()):
        reach = (jnp.dot(reach, reach, precision=highest) > 0.5).astype(f32)
    seen = reach > 0.5
    seen = lax.dynamic_slice_in_dim(seen, first_seg, local_count, 0)
    places = jnp.arange(SEG)
    key_valid = places[None, :] < lengths[:, None]
    bias = jnp.where(seen[:, :, None] & key_valid[None], 0.0, -1e30)
    bias = bias.astype(f32).reshape(local_count, segment_count * SEG)
    o1, q2, amap, bmap = delta_terms(tokens, weights, gates, own_lengths, decay_rate, head_dim)
    lin_mixed, normed = mix_rows(
        parents, amap, bmap, o1, q2, full_out, tokens, norm_gain[None, :]
    )
    return lin_mixed, attend(normed, att_q, own_kv, bias, own_lengths)


def attend_kernel(
    branches, tensors, normed_ref, q_w_ref, kv_w_ref, bias_ref, lens_ref, out_ref,
    kv, queries, accum, top, sums, far_send, far_recv, pass_send, pass_recv,
):
    me_b = lax.axis_index("branch")
    me_t = lax.axis_index("tensor")
    core = lax.rem(me_t, 2)
    partner = me_t + 1 - 2 * core
    rows = normed_ref.shape[0]
    count = rows // SEG
    half = rows // 2
    heads = q_w_ref.shape[1] // ATT_DIM

    barrier = pltpu.get_barrier_semaphore()
    for d in range(1, branches):
        pl.semaphore_signal(
            barrier, inc=1, device_id={"branch": lax.rem(me_b + d, branches)}, device_id_type=MESH
        )
    pl.semaphore_signal(barrier, inc=1, device_id={"tensor": partner}, device_id_type=MESH)

    def keys_of(branch, part):
        return pl.ds(pl.multiple_of(branch * rows + part * half, half), half)

    def far_copy(peer, source):
        return pltpu.make_async_remote_copy(
            src_ref=kv.at[keys_of(source, core)], dst_ref=kv.at[keys_of(source, core)],
            send_sem=far_send.at[peer], recv_sem=far_recv.at[source],
            device_id={"branch": peer}, device_id_type=MESH,
        )

    def pass_copy(source, part):
        return pltpu.make_async_remote_copy(
            src_ref=kv.at[keys_of(source, part)], dst_ref=kv.at[keys_of(source, part)],
            send_sem=pass_send.at[source], recv_sem=pass_recv.at[source],
            device_id={"tensor": partner}, device_id_type=MESH,
        )

    def project_half(part):
        at = pl.ds(pl.multiple_of(part * half, half), half)
        kv[keys_of(me_b, part), :] = dot1(normed_ref[at, :], kv_w_ref[...]).astype(bf16)

    project_half(core)
    pl.semaphore_wait(barrier, branches)
    for peer in range(1, branches):
        @pl.when(me_b < peer)
        def _():
            far_copy(peer, me_b).start()
    project_half(1 - core)

    scale = 1.0 / math.sqrt(ATT_DIM)

    def query_rows(j):
        return pl.ds(pl.multiple_of(j * SEG, SEG), SEG)

    def project(j, carry):
        part = dot1(normed_ref[query_rows(j), :], q_w_ref[...]).astype(bf16) * scale
        for h in range(heads):
            queries[j, h * SEG : (h + 1) * SEG, :] = (
                part[:, h * ATT_DIM : (h + 1) * ATT_DIM].astype(bf16)
            )
        return carry

    lax.fori_loop(0, count, project, 0)

    causal_row = lax.broadcasted_iota(jnp.int32, (heads * SEG, SEG), 0) % SEG
    causal_col = lax.broadcasted_iota(jnp.int32, (heads * SEG, SEG), 1)
    causal = jnp.where(causal_col <= causal_row, 0.0, -1e30)
    for j in range(count):
        seen = j + 1
        span = pl.ds(pl.multiple_of(me_b * rows, SEG), seen * SEG)
        scores = dot1(queries[j], kv[span, :ATT_DIM], NT) + bias_ref[j : j + 1, span]
        tail = scores[:, j * SEG :] + causal
        scores = tail if j == 0 else jnp.concatenate([scores[:, : j * SEG], tail], axis=1)
        best = jnp.max(scores, axis=1, keepdims=True)
        numer = jnp.exp(scores - best)
        top[j] = jnp.broadcast_to(best, top.shape[1:])
        sums[j] = jnp.broadcast_to(jnp.sum(numer, axis=1, keepdims=True), sums.shape[1:])
        accum[j] = dot1(numer.astype(bf16), kv[span, ATT_DIM:])

    def earlier(source, carry):
        far_copy(0, source).wait_recv()
        pass_copy(source, core).start()
        pass_copy(source, 1 - core).wait_recv()
        span = pl.ds(pl.multiple_of(source * rows, SEG), rows)

        def one(j, inner):
            scores = dot1(queries[j], kv[span, :ATT_DIM], NT) + bias_ref[pl.ds(j, 1), span]
            old = top[j][:, :1]
            best = jnp.maximum(old, jnp.max(scores, axis=1, keepdims=True))
            numer = jnp.exp(scores - best)
            keep = jnp.exp(old - best)
            top[j] = jnp.broadcast_to(best, top.shape[1:])
            sums[j] = sums[j] * keep + jnp.sum(numer, axis=1, keepdims=True)
            accum[j] = accum[j] * keep + dot1(numer.astype(bf16), kv[span, ATT_DIM:])
            return inner

        lax.fori_loop(0, count, one, 0)
        return carry

    lax.fori_loop(0, me_b, earlier, 0)

    def store(j, carry):
        result = accum[j] / sums[j][:, :1]
        keep = lax.broadcasted_iota(jnp.int32, (SEG, 1), 0) < lens_ref[j]
        for h in range(heads):
            out_ref[query_rows(j), h * ATT_DIM : (h + 1) * ATT_DIM] = jnp.where(
                keep, result[h * SEG : (h + 1) * SEG], 0.0
            ).astype(bf16)
        return carry

    lax.fori_loop(0, count, store, 0)

    for peer in range(1, branches):
        @pl.when(me_b < peer)
        def _():
            far_copy(peer, me_b).wait_send()

    def finish(source, carry):
        pass_copy(source, core).wait_send()
        return carry

    lax.fori_loop(0, me_b, finish, 0)


def attend(normed, att_q, own_kv, bias, own_lengths):
    branches, tensors = lax.axis_size("branch"), lax.axis_size("tensor")
    rows = normed.shape[0]
    count = rows // SEG
    heads = att_q.shape[1] // ATT_DIM
    vmem = pl.BlockSpec(memory_space=pltpu.VMEM)
    dma = pltpu.SemaphoreType.DMA
    return pl.pallas_call(
        functools.partial(attend_kernel, branches, tensors),
        in_specs=[vmem] * 4 + [pl.BlockSpec(memory_space=pltpu.SMEM)],
        out_specs=vmem,
        out_shape=jax.ShapeDtypeStruct((rows, att_q.shape[1]), bf16),
        scratch_shapes=[
            pltpu.VMEM((branches * rows, 2 * ATT_DIM), bf16),
            pltpu.VMEM((count, heads * SEG, ATT_DIM), bf16),
            pltpu.VMEM((count, heads * SEG, ATT_DIM), f32),
            pltpu.VMEM((count, heads * SEG, 128), f32),
            pltpu.VMEM((count, heads * SEG, 128), f32),
            dma((branches,)),
            dma((branches,)),
            dma((branches,)),
            dma((branches,)),
        ],
        compiler_params=pltpu.CompilerParams(
            collective_id=1, has_side_effects=True, vmem_limit_bytes=30 * MIB
        ),
    )(normed, att_q, own_kv, bias, own_lengths)


def solution(mesh):
    placed = (
        P(("rollout", "branch"), None),
        P("rollout"),
        P("rollout"),
        P(None, None, "tensor"),
        P(None, None, "tensor"),
        P("tensor"),
        P("tensor", None),
        P(),
        P(None, "tensor"),
        P(),
    )
    return jax.shard_map(
        on_device,
        mesh=mesh,
        in_specs=placed,
        out_specs=(P(("rollout", "branch", "tensor"), None), P(("rollout", "branch"), "tensor")),
        check_vma=False,
    )
```
